128 devices in a mesh: ctx: 16 (over y, x), tp: 8 (over z, core).
Axes of the slice: x: 4, y: 4, z: 4, core: 2. Of those that a mesh axis runs over, the one named last changes fastest.
Arguments:
- query_rows: bfloat16 [8192, 8192], P('ctx', 'tp'), may hold values from -6 to 6
- key_rows: bfloat16 [8192, 8192], P('ctx', 'tp'), may hold values from -6 to 6
- value_rows: bfloat16 [8192, 8192], P('ctx', 'tp'), may hold values from -6 to 6
- positions: int32 [16, 512], replicated, may hold values from -1 to 255, as said below
- filters: float32 [8192, 4096], P(('tp', 'ctx')), may hold values from -6 to 6
- bias_term: float32 [8192], P(('tp', 'ctx')), may hold values from -4 to 4
- grad_out: bfloat16 [4096, 8192], P(('ctx', 'tp')), may hold values from -6 to 6
Outputs:
- output: bfloat16 [4096, 8192], P('ctx', 'tp')
- grad_query: bfloat16 [4096, 8192], P('ctx', 'tp')
- grad_key: bfloat16 [4096, 8192], P('ctx', 'tp')
- grad_value: bfloat16 [4096, 8192], P('ctx', 'tp')
- grad_filters: float32 [8192, 4096], P(('tp', 'ctx'))
The draws below stay inside these ranges and needn't reach their ends.
Inputs may be any that keep to these rules, and one draw needn't show every extreme that they name: Entries j * 32 to (j + 1) * 32 - 1 of row i list the positions within context shard j of the rows that loader buffer i holds for shard j, or -1 for an unused row; live rows come first in such a slot and carry consecutive positions (one run of a segment). Over all buffers every position of every shard appears exactly once, and for every shard some buffer fills its whole slot of 32 rows.
All inputs are finite; a program needn't handle non-finite values.
Results may differ from the reference program's by a relative error of at most 0.0058.
Values may be sent and summed in bfloat16 or wider, within the bound.
A program may use at most 128 MiB of HBM per device.

```python
import math
import jax
import jax.numpy as jnp
from jax import lax

D = 8192
TOK_DEV = 256
TOKENS = 4096
BUF = 512
SLOT = 32
N_CTX = 16


def draw_positions(key, part):
    shards = N_CTX
    slot_rows = SLOT
    key_order, key_split = jax.random.split(key)
    orders = jax.vmap(lambda subkey: jax.random.permutation(subkey, shards))(jax.random.split(key_order, shards))
    leading = jax.random.randint(key_split, (shards, shards // 2), 0, slot_rows + 1)
    leading = leading.at[:, 0].set(slot_rows)
    run_lengths = jnp.stack([leading, slot_rows - leading], axis=2).reshape(shards, shards)
    run_starts = jnp.cumsum(run_lengths, axis=1) - run_lengths
    place_of = jnp.zeros((shards, shards), jnp.int32).at[jnp.arange(shards)[:, None], orders].set(jnp.broadcast_to(jnp.arange(shards, dtype=jnp.int32)[None, :], (shards, shards)))
    held_rows = jnp.take_along_axis(run_lengths, place_of, axis=1)
    run_start = jnp.take_along_axis(run_starts, place_of, axis=1)
    offset = jnp.arange(slot_rows, dtype=jnp.int32)
    positions_table = jnp.where(offset[None, None, :] < held_rows[:, :, None], run_start[:, :, None] + offset[None, None, :], -1)
    return jnp.transpose(positions_table, (1, 0, 2)).reshape(shards, shards * slot_rows).astype(jnp.int32)


def block_scale(rng, shape, cuts, low, largest):
    def one(dim, blocks):
        steps = jax.random.uniform(jax.random.fold_in(jax.random.fold_in(rng, 6), dim), (blocks,), jnp.float32, low / len(cuts), largest / len(cuts))
        return jnp.repeat(jnp.exp(steps), shape[dim] // blocks).reshape((-1,) + (1,) * (len(shape) - dim - 1))

    loudness = one(*cuts[0])
    for cut in cuts[1:]:
        loudness = loudness * one(*cut)
    return loudness


def scatter_about(stream_key, dims, spread, most, cuts=(), held_as=jnp.bfloat16):
    values = jax.random.normal(stream_key, dims, jnp.float32) * spread
    if len(cuts) > 0:
        values = block_scale(stream_key, dims, cuts, -0.22, 0.18) * values
    return jnp.clip(values, min=-most, max=most).astype(held_as)


def setup_inputs(seed: int = 0) -> dict:
    streams_of = jax.random.split(jax.random.key(seed), 8)
    return {
        "query_rows": scatter_about(streams_of[0], (N_CTX * BUF, D), 1.0, 6.0, ((0, 16), (1, 8))),
        "key_rows": scatter_about(streams_of[1], (N_CTX * BUF, D), 1.0, 6.0, ((0, 16), (1, 8))),
        "value_rows": scatter_about(streams_of[2], (N_CTX * BUF, D), 1.0, 6.0, ((0, 16), (1, 8))),
        "positions": draw_positions(jax.random.fold_in(streams_of[7], 71), 0),
        "filters": scatter_about(streams_of[4], (D, TOKENS), 1.0, 6.0, ((0, 128),), jnp.float32),
        "bias_term": scatter_about(streams_of[5], (D,), 1.0, 4.0, ((0, 128),), jnp.float32),
        "grad_out": scatter_about(streams_of[6], (TOKENS, D), 1.0, 6.0, ((0, 128),)),
    }


def settle_rows(rows, positions):
    column = jnp.arange(positions.shape[1], dtype=jnp.int32) // SLOT
    target = jnp.where(positions >= 0, column[None, :] * TOK_DEV + positions, TOKENS)
    target = target.reshape(-1).astype(jnp.int32)
    empty = jnp.zeros((TOKENS, rows.shape[1]), rows.dtype)
    return empty.at[target].set(rows, mode='drop')

def channel_block(pieces):
    signal, grad_conv, filters, bias_term = pieces
    length = 2 * TOKENS
    factor = 1.0 / math.sqrt(TOKENS)
    spec_signal = jnp.fft.rfft(signal, n=length, axis=1)
    spec_filter = jnp.fft.rfft(filters, n=length, axis=1)
    spec_grad = jnp.fft.rfft(grad_conv, n=length, axis=1)
    forward_conv = jnp.fft.irfft(spec_filter * spec_signal, n=length, axis=1)[:, :TOKENS]
    backward_conv = jnp.fft.irfft(jnp.conj(spec_filter) * spec_grad, n=length, axis=1)[:, :TOKENS]
    filter_corr = jnp.fft.irfft(jnp.conj(spec_signal) * spec_grad, n=length, axis=1)[:, :TOKENS]
    conv_out = bias_term[:, None] * signal + factor * forward_conv
    grad_signal = bias_term[:, None] * grad_conv + factor * backward_conv
    return (conv_out, grad_signal, factor * filter_corr)

def reference(query_rows, key_rows, value_rows, positions, filters, bias_term, grad_out):
    query_seq = settle_rows(query_rows, positions)
    key_seq = settle_rows(key_rows, positions)
    value_seq = settle_rows(value_rows, positions)
    signal = (key_seq.astype(jnp.float32) * value_seq.astype(jnp.float32)).astype(jnp.bfloat16)
    grad_conv = (grad_out.astype(jnp.float32) * query_seq.astype(jnp.float32)).astype(jnp.bfloat16)
    width_block = min(256, D)
    blocks_count = D // width_block

    def stacked(array):
        return array.astype(jnp.float32).T.reshape(blocks_count, width_block, TOKENS)
    conv_out, grad_signal, grad_filters = lax.map(channel_block, (stacked(signal), stacked(grad_conv), filters.reshape(blocks_count, width_block, TOKENS), bias_term.reshape(blocks_count, width_block)))
    conv_out = conv_out.reshape(D, TOKENS).T.astype(jnp.bfloat16)
    grad_signal = grad_signal.reshape(D, TOKENS).T.astype(jnp.bfloat16)
    grad_filters = grad_filters.reshape(D, TOKENS)
    output = (query_seq.astype(jnp.float32) * conv_out.astype(jnp.float32)).astype(jnp.bfloat16)
    grad_query = (grad_out.astype(jnp.float32) * conv_out.astype(jnp.float32)).astype(jnp.bfloat16)
    grad_key = (grad_signal.astype(jnp.float32) * value_seq.astype(jnp.float32)).astype(jnp.bfloat16)
    grad_value = (grad_signal.astype(jnp.float32) * key_seq.astype(jnp.float32)).astype(jnp.bfloat16)
    return (output, grad_query, grad_key, grad_value, grad_filters)
```

```python
import math

import jax
import jax.numpy as jnp
import numpy as np
from jax import lax
from jax.experimental import pallas as pl
from jax.experimental.pallas import tpu as pltpu
from jax.sharding import PartitionSpec as P

MESH = pl.DeviceIdType.MESH
BF = jnp.bfloat16
F32 = jnp.float32


def split_bf16(table):
    high = table.astype(jnp.bfloat16)
    low = (table - high.astype(np.float64)).astype(jnp.bfloat16)
    return high, low


def make_tables(shards, tokens):
    length = 2 * shards * tokens
    r = np.arange(tokens)
    inner = 2.0 * math.pi * ((r[:, None] * r[None, :]) % tokens) / tokens
    cos, sin = np.cos(inner), np.sin(inner)
    forward = np.block([[cos, -sin], [sin, cos]])
    backward = np.block([[cos, sin], [-sin, cos]])
    k = np.arange(shards + 1)
    twist = 2.0 * math.pi * (k[:, None] * r[None, :]) / length
    return (
        split_bf16(forward),
        split_bf16(backward),
        np.cos(twist).astype(np.float32),
        np.sin(twist).astype(np.float32),
    )


def real_dft_padded(xs):
    half = len(xs)
    if half == 1:
        return [(xs[0], None), (xs[0], None)]
    even = real_dft_padded(xs[0::2])
    odd = real_dft_padded(xs[1::2])
    out = [None] * (half + 1)
    out[0] = (even[0][0] + odd[0][0], None)
    out[half] = (even[0][0] - odd[0][0], None)
    mid = half // 2
    for k in range(1, mid):
        angle = math.pi * k / half
        c, s = math.cos(angle), math.sin(angle)
        o_re, o_im = odd[k]
        t_re = o_re * c + o_im * s
        t_im = o_im * c - o_re * s
        e_re, e_im = even[k]
        out[k] = (e_re + t_re, e_im + t_im)
        out[half - k] = (e_re - t_re, t_im - e_im)
    out[mid] = (even[mid][0], -odd[mid][0])
    return out


def real_inverse_half(bins):
    half = len(bins) - 1
    if half == 1:
        return [bins[0][0] + bins[1][0]]
    mid = half // 2
    even = [None] * (mid + 1)
    odd = [None] * (mid + 1)
    even[0] = (bins[0][0] + bins[half][0], None)
    odd[0] = (bins[0][0] - bins[half][0], None)
    for k in range(1, mid):
        angle = math.pi * k / half
        c, s = math.cos(angle), math.sin(angle)
        a_re, a_im = bins[k]
        b_re, b_im = bins[half - k]
        even[k] = (a_re + b_re, a_im - b_im)
        d_re, d_im = a_re - b_re, a_im + b_im
        odd[k] = (d_re * c - d_im * s, d_im * c + d_re * s)
    m_re, m_im = bins[mid]
    even[mid] = (m_re + m_re, None)
    odd[mid] = (-(m_im + m_im), None)
    y_even = real_inverse_half(even)
    y_odd = real_inverse_half(odd)
    out = [None] * half
    out[0::2] = y_even
    out[1::2] = y_odd
    return out


def kernel_body(
    sizes,
    q_hbm, k_hbm, v_hbm, g_hbm, f_hbm, wf_hi_hbm, wf_lo_hbm, wi_hi_hbm, wi_lo_hbm,
    slot_ref, bias_ref, cos_ref, sin_ref,
    out_ref, gq_ref, gk_ref, gv_ref, gf_ref,
    rq, rk, rv, gtok, f_buf, wf_hi, wf_lo, wi_hi, wi_lo,
    hot, q_seq, k_seq, v_seq, sig_t, gc_t, sig_in, gc_in,
    l_hi, l_lo, spec_f, spec_s, spec_g, z_buf,
    conv_o, gs_o, conv_t, gs_t,
    recv_sem, send_sem, local_sem,
):
    n_ctx, n_tp, tok, slot, chan = sizes
    side = 4
    width = n_ctx * chan
    me = lax.axis_index("ctx")
    my_tp = lax.axis_index("tp")
    my_y, my_x = me // side, me % side
    factor = 1.0 / math.sqrt(n_ctx * tok)
    inv_len = 1.0 / (2 * n_ctx * tok)
    bins = n_ctx + 1

    def partner(o):
        return ((my_y + o // side) % side) * side + (my_x + o % side) % side

    def each_partner(fn):
        lax.fori_loop(1, n_ctx, lambda o, c: (fn(partner(o)), c)[1], 0)

    loads = [
        pltpu.make_async_copy(src, dst, local_sem.at[n])
        for n, (src, dst) in enumerate(
            ((f_hbm, f_buf), (wf_hi_hbm, wf_hi), (wf_lo_hbm, wf_lo), (wi_hi_hbm, wi_hi), (wi_lo_hbm, wi_lo))
        )
    ]
    for copy in loads:
        copy.start()

    barrier = pltpu.get_barrier_semaphore()
    each_partner(
        lambda d: pl.semaphore_signal(barrier, inc=1, device_id=(d, my_tp), device_id_type=MESH)
    )
    lax.fori_loop(
        1,
        n_tp,
        lambda o, c: (
            pl.semaphore_signal(
                barrier, inc=1, device_id=(me, (my_tp + o) % n_tp), device_id_type=MESH
            ),
            c,
        )[1],
        0,
    )
    pl.semaphore_wait(barrier, n_ctx + n_tp - 2)

    def send_rows(src, dst, n):
        def one(d):
            pltpu.make_async_remote_copy(
                src_ref=src.at[pl.ds(pl.multiple_of(d * slot, slot), slot), :],
                dst_ref=dst.at[pl.ds(pl.multiple_of(me * slot, slot), slot), :],
                send_sem=send_sem.at[n],
                recv_sem=recv_sem.at[n],
                device_id=(d, my_tp),
                device_id_type=MESH,
            ).start()

        own = pl.ds(pl.multiple_of(me * slot, slot), slot)
        pltpu.make_async_copy(src.at[own, :], dst.at[own, :], recv_sem.at[n]).start()
        each_partner(one)

    send_rows(k_hbm, rk, 0)
    send_rows(v_hbm, rv, 1)

    def send_grad(o, carry):
        d = (my_tp + o) % n_tp
        pltpu.make_async_remote_copy(
            src_ref=g_hbm.at[:, pl.ds(pl.multiple_of(d * width, width), width)],
            dst_ref=gtok.at[pl.ds(pl.multiple_of(my_tp * slot, slot), slot), :],
            send_sem=send_sem.at[3],
            recv_sem=recv_sem.at[3],
            device_id=(me, d),
            device_id_type=MESH,
        ).start()
        return carry

    pltpu.make_async_copy(
        g_hbm.at[:, pl.ds(pl.multiple_of(my_tp * width, width), width)],
        gtok.at[pl.ds(pl.multiple_of(my_tp * slot, slot), slot), :],
        recv_sem.at[3],
    ).start()
    lax.fori_loop(1, n_tp, send_grad, 0)
    send_rows(q_hbm, rq, 2)

    hot[...] = jnp.where(
        slot_ref[...] == lax.broadcasted_iota(jnp.int32, hot.shape, 0), 1.0, 0.0
    ).astype(BF)

    row_step, lane_step = 16, 128
    halves = tok // lane_step
    pieces = (chan // row_step) * halves

    def place(it):
        rows = pl.multiple_of((it // halves) * row_step, row_step)
        lanes = pl.multiple_of((it % halves) * lane_step, lane_step)
        return rows, lanes

    def put_split(row, lane, value):
        high = value.astype(BF)
        at = (pl.ds(pl.multiple_of(row, row_step), row_step), pl.ds(pl.multiple_of(lane, lane_step), lane_step))
        l_hi[at] = high
        l_lo[at] = (value - high.astype(F32)).astype(BF)

    def forward_outer(load):
        def step(it, carry):
            rows, lanes = place(it)
            spectrum = real_dft_padded([load(j, rows, lanes) for j in range(n_ctx)])
            for k in range(bins):
                re, im = spectrum[k]
                if k == 0:
                    put_split(rows, lanes, re)
                    put_split(rows, tok + lanes, jnp.zeros_like(re))
                    continue
                c = cos_ref[k : k + 1, pl.ds(lanes, lane_step)]
                s = sin_ref[k : k + 1, pl.ds(lanes, lane_step)]
                if im is None:
                    t_re, t_im = re * c, -(re * s)
                else:
                    t_re, t_im = re * c + im * s, im * c - re * s
                put_split(k * chan + rows, lanes, t_re)
                put_split(k * chan + rows, tok + lanes, t_im)
            return carry

        lax.fori_loop(0, pieces, step, 0)

    total_rows = bins * chan
    block_rows = total_rows // 4

    def inner(high, low, dest):
        def step(m, carry):
            at = pl.ds(pl.multiple_of(m * block_rows, row_step), block_rows)
            a, b = l_hi[at, :], l_lo[at, :]
            dest[at, :] = (
                jnp.dot(a, high[...], preferred_element_type=F32)
                + jnp.dot(a, low[...], preferred_element_type=F32)
                + jnp.dot(b, high[...], preferred_element_type=F32)
            )
            return carry

        lax.fori_loop(0, 4, step, 0)

    def multiply(one, two, conjugate_one):
        def step(m, carry):
            row = m * row_step
            at = pl.ds(pl.multiple_of(row, row_step), row_step)
            for lane in range(0, tok, lane_step):
                re_at, im_at = slice(lane, lane + lane_step), slice(tok + lane, tok + lane + lane_step)
                a, b = one[at, re_at], one[at, im_at]
                c, d = two[at, re_at], two[at, im_at]
                if conjugate_one:
                    re, im = a * c + b * d, a * d - b * c
                else:
                    re, im = a * c - b * d, a * d + b * c
                put_split(row, lane, re)
                put_split(row, tok + lane, im)
            return carry

        lax.fori_loop(0, total_rows // row_step, step, 0)

    def inverse_outer(store):
        def step(it, carry):
            rows, lanes = place(it)
            spectrum = []
            for k in range(bins):
                at = pl.ds(pl.multiple_of(k * chan + rows, row_step), row_step)
                re = z_buf[at, pl.ds(lanes, lane_step)]
                if k == 0:
                    spectrum.append((re, None))
                    continue
                im = z_buf[at, pl.ds(pl.multiple_of(tok + lanes, lane_step), lane_step)]
                c = cos_ref[k : k + 1, pl.ds(lanes, lane_step)]
                s = sin_ref[k : k + 1, pl.ds(lanes, lane_step)]
                if k == n_ctx:
                    spectrum.append((re * c - im * s, None))
                else:
                    spectrum.append((re * c - im * s, im * c + re * s))
            for j, y in enumerate(real_inverse_half(spectrum)):
                store(j, rows, lanes, y * (factor * inv_len))
            return carry

        lax.fori_loop(0, pieces, step, 0)

    for copy in loads:
        copy.wait()
    forward_outer(
        lambda j, rows, lanes: f_buf[
            pl.ds(rows, row_step), pl.ds(pl.multiple_of(j * tok + lanes, lane_step), lane_step)
        ]
    )
    inner(wf_hi, wf_lo, spec_f)

    def wait_all(buf, n):
        pltpu.make_async_copy(buf, buf, recv_sem.at[n]).wait()

    def settled(rows_ref, cols):
        return jnp.dot(hot[...], rows_ref[:, cols], preferred_element_type=F32)

    group = side * chan

    def send_channels(src, dst, n, y):
        def one(dx, carry):
            d = y * side + (my_x + dx) % side
            at = pl.ds(pl.multiple_of(d * chan, chan), chan)
            pl.when(d != me)(
                lambda: pltpu.make_async_remote_copy(
                    src_ref=src.at[at, :],
                    dst_ref=dst.at[me],
                    send_sem=send_sem.at[n],
                    recv_sem=recv_sem.at[n],
                    device_id=(d, my_tp),
                    device_id_type=MESH,
                ).start()
            )
            return carry

        lax.fori_loop(0, side, one, 0)

    def send_own_channels(src, dst, n):
        at = pl.ds(pl.multiple_of(me * chan, chan), chan)
        pltpu.make_async_copy(src.at[at, :], dst.at[me], recv_sem.at[n]).start()

    wait_all(rk, 0)
    wait_all(rv, 1)

    def signal_step(i, carry):
        y = (my_y + i) % side
        cols = pl.ds(pl.multiple_of(y * group, group), group)
        key = settled(rk, cols)
        value = settled(rv, cols)
        k_seq[:, cols] = key.astype(BF)
        v_seq[:, cols] = value.astype(BF)
        sig_t[cols, :] = (key * value).T.astype(BF)
        send_channels(sig_t, sig_in, 4, y)
        return carry

    lax.fori_loop(0, side, signal_step, 0)
    send_own_channels(sig_t, sig_in, 4)

    wait_all(rq, 2)
    wait_all(gtok, 3)

    def grad_step(i, carry):
        y = (my_y + i) % side
        cols = pl.ds(pl.multiple_of(y * group, group), group)
        query = settled(rq, cols)
        q_seq[:, cols] = query.astype(BF)
        gc_t[cols, :] = (query * gtok[:, cols].astype(F32)).T.astype(BF)
        send_channels(gc_t, gc_in, 5, y)
        return carry

    lax.fori_loop(0, side, grad_step, 0)
    send_own_channels(gc_t, gc_in, 5)

    def send_tokens(src, dst, n):
        at = pl.ds(pl.multiple_of(me * chan, chan), chan)

        def one(d):
            pltpu.make_async_remote_copy(
                src_ref=src.at[d],
                dst_ref=dst.at[at, :],
                send_sem=send_sem.at[n],
                recv_sem=recv_sem.at[n],
                device_id=(d, my_tp),
                device_id_type=MESH,
            ).start()

        pltpu.make_async_copy(src.at[me], dst.at[at, :], recv_sem.at[n]).start()
        each_partner(one)

    def piece(buf, j, rows, lanes):
        return buf[j, pl.ds(rows, row_step), pl.ds(lanes, lane_step)].astype(F32)

    def store_with_bias(direct, dest):
        def store(j, rows, lanes, y):
            bias = bias_ref[pl.ds(rows, row_step), :]
            dest[j, pl.ds(rows, row_step), pl.ds(lanes, lane_step)] = (
                bias * piece(direct, j, rows, lanes) + y
            ).astype(BF)

        return store

    wait_all(sig_in, 4)
    forward_outer(lambda j, rows, lanes: piece(sig_in, j, rows, lanes))
    inner(wf_hi, wf_lo, spec_s)
    multiply(spec_f, spec_s, False)
    inner(wi_hi, wi_lo, z_buf)
    inverse_outer(store_with_bias(sig_in, conv_o))
    send_tokens(conv_o, conv_t, 6)

    wait_all(gc_in, 5)
    forward_outer(lambda j, rows, lanes: piece(gc_in, j, rows, lanes))
    inner(wf_hi, wf_lo, spec_g)
    multiply(spec_f, spec_g, True)
    inner(wi_hi, wi_lo, z_buf)
    inverse_outer(store_with_bias(gc_in, gs_o))
    send_tokens(gs_o, gs_t, 7)

    multiply(spec_s, spec_g, True)
    inner(wi_hi, wi_lo, z_buf)

    def store_filter(j, rows, lanes, y):
        gf_ref[pl.ds(rows, row_step), pl.ds(pl.multiple_of(j * tok + lanes, lane_step), lane_step)] = y

    inverse_outer(store_filter)

    wait_all(conv_t, 6)

    def output_step(i, carry):
        cols = pl.ds(pl.multiple_of(i * group, group), group)
        conv = conv_t[cols, :].astype(F32).T
        out_ref[:, cols] = (q_seq[:, cols].astype(F32) * conv).astype(BF)
        gq_ref[:, cols] = (gtok[:, cols].astype(F32) * conv).astype(BF)
        return carry

    lax.fori_loop(0, side, output_step, 0)

    wait_all(gs_t, 7)

    def gradient_step(i, carry):
        cols = pl.ds(pl.multiple_of(i * group, group), group)
        grad = gs_t[cols, :].astype(F32).T
        gk_ref[:, cols] = (grad * v_seq[:, cols].astype(F32)).astype(BF)
        gv_ref[:, cols] = (grad * k_seq[:, cols].astype(F32)).astype(BF)
        return carry

    lax.fori_loop(0, side, gradient_step, 0)

    def wait_sent(buf, n):
        pltpu.make_async_copy(buf, buf, send_sem.at[n]).wait()

    rows_sent = pl.ds(0, (n_ctx - 1) * slot)
    wait_sent(rk.at[rows_sent, :], 0)
    wait_sent(rv.at[rows_sent, :], 1)
    wait_sent(rq.at[rows_sent, :], 2)
    wait_sent(gtok.at[pl.ds(0, (n_tp - 1) * slot), :], 3)
    parts_sent = pl.ds(0, n_ctx - 1)
    wait_sent(sig_in.at[parts_sent], 4)
    wait_sent(gc_in.at[parts_sent], 5)
    wait_sent(conv_o.at[parts_sent], 6)
    wait_sent(gs_o.at[parts_sent], 7)


def solution(mesh):
    n_ctx, n_tp = mesh.shape["ctx"], mesh.shape["tp"]

    def per_device(query_rows, key_rows, value_rows, positions, filters, bias_term, grad_out):
        width = query_rows.shape[1]
        slot = query_rows.shape[0] // n_ctx
        tok = grad_out.shape[0] * n_tp
        chan = filters.shape[0]
        (wf_hi, wf_lo), (wi_hi, wi_lo), cos, sin = make_tables(n_ctx, tok)
        own = lax.dynamic_slice_in_dim(positions, lax.axis_index("ctx") * slot, slot, 1)
        own = own.reshape(1, n_ctx * slot)
        bins = n_ctx + 1
        vm = pltpu.VMEM
        rows_bf = vm((n_ctx * slot, width), BF)
        seq = vm((tok, width), BF)
        seq_t = vm((width, tok), BF)
        parts = vm((n_ctx, chan, tok), BF)
        spec = vm((bins * chan, 2 * tok), F32)
        half_spec = vm((bins * chan, 2 * tok), BF)
        table = vm((2 * tok, 2 * tok), BF)
        any_spec = pl.BlockSpec(memory_space=pl.ANY)
        vmem_spec = pl.BlockSpec(memory_space=pltpu.VMEM)
        seq_out = jax.ShapeDtypeStruct((tok, width), BF)

        def body(*refs):
            kernel_body((n_ctx, n_tp, tok, slot, chan), *refs)

        return pl.pallas_call(
            body,
            out_shape=(seq_out, seq_out, seq_out, seq_out, jax.ShapeDtypeStruct(filters.shape, F32)),
            in_specs=[any_spec] * 9 + [vmem_spec] * 4,
            out_specs=(vmem_spec,) * 5,
            scratch_shapes=[
                rows_bf, rows_bf, rows_bf, seq, vm(filters.shape, F32), table, table, table, table,
                vm((tok, n_ctx * slot), BF), seq, seq, seq, seq_t, seq_t, parts, parts,
                half_spec, half_spec, spec, spec, spec, spec,
                parts, parts, seq_t, seq_t,
                pltpu.SemaphoreType.DMA((8,)),
                pltpu.SemaphoreType.DMA((8,)),
                pltpu.SemaphoreType.DMA((5,)),
            ],
            compiler_params=pltpu.CompilerParams(
                collective_id=0, has_side_effects=True, vmem_limit_bytes=56 * 1024 * 1024
            ),
        )(
            query_rows, key_rows, value_rows, grad_out, filters,
            wf_hi, wf_lo, wi_hi, wi_lo,
            own, bias_term.reshape(chan, 1), cos, sin,
        )

    in_specs = (
        P("ctx", "tp"),
        P("ctx", "tp"),
        P("ctx", "tp"),
        P(),
        P(("tp", "ctx"), None),
        P(("tp", "ctx")),
        P(("ctx", "tp"), None),
    )
    out_specs = (
        P("ctx", "tp"),
        P("ctx", "tp"),
        P("ctx", "tp"),
        P("ctx", "tp"),
        P(("tp", "ctx"), None),
    )
    return jax.shard_map(
        per_device, mesh=mesh, in_specs=in_specs, out_specs=out_specs, check_vma=False
    )
```

```python
import math

import jax
import jax.numpy as jnp
import numpy as np
from jax import lax
from jax.experimental import pallas as pl
from jax.experimental.pallas import tpu as pltpu
from jax.sharding import PartitionSpec as P

MESH = pl.DeviceIdType.MESH
BF = jnp.bfloat16
F32 = jnp.float32
FAR_FIRST = (10, 5, 15, 13, 7, 14, 6, 11, 9, 2, 8, 1, 12, 3, 4)


def split_bf16(table):
    high = table.astype(jnp.bfloat16)
    low = (table - high.astype(np.float64)).astype(jnp.bfloat16)
    return high, low


def make_tables(shards, tokens):
    length = 2 * shards * tokens
    r = np.arange(tokens)
    inner = 2.0 * math.pi * ((r[:, None] * r[None, :]) % tokens) / tokens
    cos, sin = np.cos(inner), np.sin(inner)
    forward = np.block([[cos, -sin], [sin, cos]])
    backward = np.block([[cos, sin], [-sin, cos]])
    k = np.arange(shards + 1)
    twist = 2.0 * math.pi * (k[:, None] * r[None, :]) / length
    return (
        split_bf16(forward),
        split_bf16(backward),
        np.cos(twist).astype(np.float32),
        np.sin(twist).astype(np.float32),
    )


def real_dft_padded(xs):
    half = len(xs)
    if half == 1:
        return [(xs[0], None), (xs[0], None)]
    even = real_dft_padded(xs[0::2])
    odd = real_dft_padded(xs[1::2])
    out = [None] * (half + 1)
    out[0] = (even[0][0] + odd[0][0], None)
    out[half] = (even[0][0] - odd[0][0], None)
    mid = half // 2
    for k in range(1, mid):
        angle = math.pi * k / half
        c, s = math.cos(angle), math.sin(angle)
        o_re, o_im = odd[k]
        t_re = o_re * c + o_im * s
        t_im = o_im * c - o_re * s
        e_re, e_im = even[k]
        out[k] = (e_re + t_re, e_im + t_im)
        out[half - k] = (e_re - t_re, t_im - e_im)
    out[mid] = (even[mid][0], -odd[mid][0])
    return out


def real_inverse_half(bins):
    half = len(bins) - 1
    if half == 1:
        return [bins[0][0] + bins[1][0]]
    mid = half // 2
    even = [None] * (mid + 1)
    odd = [None] * (mid + 1)
    even[0] = (bins[0][0] + bins[half][0], None)
    odd[0] = (bins[0][0] - bins[half][0], None)
    for k in range(1, mid):
        angle = math.pi * k / half
        c, s = math.cos(angle), math.sin(angle)
        a_re, a_im = bins[k]
        b_re, b_im = bins[half - k]
        even[k] = (a_re + b_re, a_im - b_im)
        d_re, d_im = a_re - b_re, a_im + b_im
        odd[k] = (d_re * c - d_im * s, d_im * c + d_re * s)
    m_re, m_im = bins[mid]
    even[mid] = (m_re + m_re, None)
    odd[mid] = (-(m_im + m_im), None)
    y_even = real_inverse_half(even)
    y_odd = real_inverse_half(odd)
    out = [None] * half
    out[0::2] = y_even
    out[1::2] = y_odd
    return out


def kernel_body(
    sizes,
    q_hbm, k_hbm, v_hbm, g_hbm, f_hbm, wf_hi_hbm, wf_lo_hbm, wi_hi_hbm, wi_lo_hbm,
    slot_ref, bias_ref, cos_ref, sin_ref,
    q_out, g_out, k_out, v_out, conv_t, gs_t, f_out,
    rq, rk, rv, gtok, f_buf, wf_hi, wf_lo, wi_hi, wi_lo,
    hot, q_seq, k_seq, v_seq, sig_t, gc_t, sig_in, gc_in,
    l_hi, l_lo, spec_f, spec_s, spec_g, z_buf,
    conv_o, gs_o, gf_ref,
    recv_sem, send_sem, local_sem, out_sem,
):
    n_ctx, n_tp, tok, slot, chan = sizes
    side = 4
    width = n_ctx * chan
    me = lax.axis_index("ctx")
    my_tp = lax.axis_index("tp")
    my_y, my_x = me // side, me % side
    factor = 1.0 / math.sqrt(n_ctx * tok)
    inv_len = 1.0 / (2 * n_ctx * tok)
    bins = n_ctx + 1

    def partner(o):
        return ((my_y + o // side) % side) * side + (my_x + o % side) % side

    def each_partner(fn):
        for o in FAR_FIRST:
            fn(partner(o))

    loads = [
        pltpu.make_async_copy(src, dst, local_sem.at[n])
        for n, (src, dst) in enumerate(
            ((f_hbm, f_buf), (wf_hi_hbm, wf_hi), (wf_lo_hbm, wf_lo), (wi_hi_hbm, wi_hi), (wi_lo_hbm, wi_lo))
        )
    ]
    for copy in loads:
        copy.start()

    barrier = pltpu.get_barrier_semaphore()
    each_partner(
        lambda d: pl.semaphore_signal(barrier, inc=1, device_id=(d, my_tp), device_id_type=MESH)
    )
    lax.fori_loop(
        1,
        n_tp,
        lambda o, c: (
            pl.semaphore_signal(
                barrier, inc=1, device_id=(me, (my_tp + o) % n_tp), device_id_type=MESH
            ),
            c,
        )[1],
        0,
    )
    pl.semaphore_wait(barrier, n_ctx + n_tp - 2)

    def send_rows(src, dst, n):
        def one(d):
            pltpu.make_async_remote_copy(
                src_ref=src.at[pl.ds(pl.multiple_of(d * slot, slot), slot), :],
                dst_ref=dst.at[pl.ds(pl.multiple_of(me * slot, slot), slot), :],
                send_sem=send_sem.at[n],
                recv_sem=recv_sem.at[n],
                device_id=(d, my_tp),
                device_id_type=MESH,
            ).start()

        own = pl.ds(pl.multiple_of(me * slot, slot), slot)
        pltpu.make_async_copy(src.at[own, :], dst.at[own, :], recv_sem.at[n]).start()
        each_partner(one)

    send_rows(k_hbm, rk, 0)
    send_rows(v_hbm, rv, 1)

    def send_grad(o, carry):
        d = (my_tp + o) % n_tp
        pltpu.make_async_remote_copy(
            src_ref=g_hbm.at[:, pl.ds(pl.multiple_of(d * width, width), width)],
            dst_ref=gtok.at[pl.ds(pl.multiple_of(my_tp * slot, slot), slot), :],
            send_sem=send_sem.at[3],
            recv_sem=recv_sem.at[3],
            device_id=(me, d),
            device_id_type=MESH,
        ).start()
        return carry

    pltpu.make_async_copy(
        g_hbm.at[:, pl.ds(pl.multiple_of(my_tp * width, width), width)],
        gtok.at[pl.ds(pl.multiple_of(my_tp * slot, slot), slot), :],
        recv_sem.at[3],
    ).start()
    lax.fori_loop(1, n_tp, send_grad, 0)
    send_rows(q_hbm, rq, 2)

    hot[...] = jnp.where(
        slot_ref[...] == lax.broadcasted_iota(jnp.int32, hot.shape, 0), 1.0, 0.0
    ).astype(BF)

    row_step, lane_step = 16, 128
    halves = tok // lane_step
    pieces = (chan // row_step) * halves

    def place(it):
        rows = pl.multiple_of((it // halves) * row_step, row_step)
        lanes = pl.multiple_of((it % halves) * lane_step, lane_step)
        return rows, lanes

    def put_split(row, lane, value, exact):
        high = value.astype(BF)
        at = (pl.ds(pl.multiple_of(row, row_step), row_step), pl.ds(pl.multiple_of(lane, lane_step), lane_step))
        l_hi[at] = high
        if exact:
            l_lo[at] = (value - high.astype(F32)).astype(BF)

    def forward_outer(load, exact):
        def step(it, carry):
            rows, lanes = place(it)
            spectrum = real_dft_padded([load(j, rows, lanes) for j in range(n_ctx)])
            for k in range(bins):
                re, im = spectrum[k]
                if k == 0:
                    put_split(rows, lanes, re, exact)
                    put_split(rows, tok + lanes, jnp.zeros_like(re), exact)
                    continue
                c = cos_ref[k : k + 1, pl.ds(lanes, lane_step)]
                s = sin_ref[k : k + 1, pl.ds(lanes, lane_step)]
                if im is None:
                    t_re, t_im = re * c, -(re * s)
                else:
                    t_re, t_im = re * c + im * s, im * c - re * s
                put_split(k * chan + rows, lanes, t_re, exact)
                put_split(k * chan + rows, tok + lanes, t_im, exact)
            return carry

        lax.fori_loop(0, pieces, step, 0)

    total_rows = bins * chan
    block_rows = total_rows // 4

    def inner(high, low, dest, exact):
        def step(m, carry):
            at = pl.ds(pl.multiple_of(m * block_rows, row_step), block_rows)
            a = l_hi[at, :]
            total = jnp.dot(a, high[...], preferred_element_type=F32)
            total += jnp.dot(a, low[...], preferred_element_type=F32)
            if exact:
                total += jnp.dot(l_lo[at, :], high[...], preferred_element_type=F32)
            dest[at, :] = total
            return carry

        lax.fori_loop(0, 4, step, 0)

    def multiply(one, two, conjugate_one, exact):
        def step(m, carry):
            row = m * row_step
            at = pl.ds(pl.multiple_of(row, row_step), row_step)
            for lane in range(0, tok, lane_step):
                re_at, im_at = slice(lane, lane + lane_step), slice(tok + lane, tok + lane + lane_step)
                a, b = one[at, re_at], one[at, im_at]
                c, d = two[at, re_at], two[at, im_at]
                if conjugate_one:
                    re, im = a * c + b * d, a * d - b * c
                else:
                    re, im = a * c - b * d, a * d + b * c
                put_split(row, lane, re, exact)
                put_split(row, tok + lane, im, exact)
            return carry

        lax.fori_loop(0, total_rows // row_step, step, 0)

    def inverse_outer(store):
        def step(it, carry):
            rows, lanes = place(it)
            spectrum = []
            for k in range(bins):
                at = pl.ds(pl.multiple_of(k * chan + rows, row_step), row_step)
                re = z_buf[at, pl.ds(lanes, lane_step)]
                if k == 0:
                    spectrum.append((re, None))
                    continue
                im = z_buf[at, pl.ds(pl.multiple_of(tok + lanes, lane_step), lane_step)]
                c = cos_ref[k : k + 1, pl.ds(lanes, lane_step)]
                s = sin_ref[k : k + 1, pl.ds(lanes, lane_step)]
                if k == n_ctx:
                    spectrum.append((re * c - im * s, None))
                else:
                    spectrum.append((re * c - im * s, im * c + re * s))
            for j, y in enumerate(real_inverse_half(spectrum)):
                store(j, rows, lanes, y * (factor * inv_len))
            return carry

        lax.fori_loop(0, pieces, step, 0)

    for copy in loads:
        copy.wait()
    forward_outer(
        lambda j, rows, lanes: f_buf[
            pl.ds(rows, row_step), pl.ds(pl.multiple_of(j * tok + lanes, lane_step), lane_step)
        ],
        True,
    )
    inner(wf_hi, wf_lo, spec_f, True)

    def wait_all(buf, n):
        pltpu.make_async_copy(buf, buf, recv_sem.at[n]).wait()

    def hand_out(src, dst, n):
        pltpu.make_async_copy(src, dst, out_sem.at[n]).start()

    def settled(rows_ref, cols):
        return jnp.dot(hot[...], rows_ref[:, cols], preferred_element_type=F32)

    group = side * chan

    def send_channels(src, dst, n, y):
        def one(dx, carry):
            d = y * side + (my_x + dx) % side
            at = pl.ds(pl.multiple_of(d * chan, chan), chan)
            pl.when(d != me)(
                lambda: pltpu.make_async_remote_copy(
                    src_ref=src.at[at, :],
                    dst_ref=dst.at[me],
                    send_sem=send_sem.at[n],
                    recv_sem=recv_sem.at[n],
                    device_id=(d, my_tp),
                    device_id_type=MESH,
                ).start()
            )
            return carry

        lax.fori_loop(0, side, one, 0)

    def send_own_channels(src, dst, n):
        at = pl.ds(pl.multiple_of(me * chan, chan), chan)
        pltpu.make_async_copy(src.at[at, :], dst.at[me], recv_sem.at[n]).start()

    wait_all(rk, 0)
    wait_all(rv, 1)

    def signal_step(i, carry):
        y = (my_y + i) % side
        cols = pl.ds(pl.multiple_of(y * group, group), group)
        key = settled(rk, cols)
        value = settled(rv, cols)
        k_seq[:, cols] = key.astype(BF)
        v_seq[:, cols] = value.astype(BF)
        sig_t[cols, :] = (key * value).T.astype(BF)
        send_channels(sig_t, sig_in, 4, y)
        return carry

    lax.fori_loop(0, side, signal_step, 0)
    send_own_channels(sig_t, sig_in, 4)
    hand_out(k_seq, k_out, 0)
    hand_out(v_seq, v_out, 1)

    wait_all(rq, 2)
    wait_all(gtok, 3)

    def grad_step(i, carry):
        y = (my_y + i) % side
        cols = pl.ds(pl.multiple_of(y * group, group), group)
        query = settled(rq, cols)
        q_seq[:, cols] = query.astype(BF)
        gc_t[cols, :] = (query * gtok[:, cols].astype(F32)).T.astype(BF)
        send_channels(gc_t, gc_in, 5, y)
        return carry

    lax.fori_loop(0, side, grad_step, 0)
    send_own_channels(gc_t, gc_in, 5)
    hand_out(q_seq, q_out, 2)
    hand_out(gtok, g_out, 3)

    def send_tokens(src, dst, n):
        at = pl.ds(pl.multiple_of(me * chan, chan), chan)

        def one(d):
            pltpu.make_async_remote_copy(
                src_ref=src.at[d],
                dst_ref=dst.at[at, :],
                send_sem=send_sem.at[n],
                recv_sem=recv_sem.at[n],
                device_id=(d, my_tp),
                device_id_type=MESH,
            ).start()

        pltpu.make_async_copy(src.at[me], dst.at[at, :], recv_sem.at[n]).start()
        each_partner(one)

    def piece(buf, j, rows, lanes):
        return buf[j, pl.ds(rows, row_step), pl.ds(lanes, lane_step)].astype(F32)

    def store_with_bias(direct, dest):
        def store(j, rows, lanes, y):
            bias = bias_ref[pl.ds(rows, row_step), :]
            dest[j, pl.ds(rows, row_step), pl.ds(lanes, lane_step)] = (
                bias * piece(direct, j, rows, lanes) + y
            ).astype(BF)

        return store

    wait_all(sig_in, 4)
    forward_outer(lambda j, rows, lanes: piece(sig_in, j, rows, lanes), False)
    inner(wf_hi, wf_lo, spec_s, False)
    multiply(spec_f, spec_s, False, False)
    inner(wi_hi, wi_lo, z_buf, False)
    inverse_outer(store_with_bias(sig_in, conv_o))
    send_tokens(conv_o, conv_t, 6)

    wait_all(gc_in, 5)
    forward_outer(lambda j, rows, lanes: piece(gc_in, j, rows, lanes), False)
    inner(wf_hi, wf_lo, spec_g, False)
    multiply(spec_f, spec_g, True, False)
    inner(wi_hi, wi_lo, z_buf, False)
    inverse_outer(store_with_bias(gc_in, gs_o))
    send_tokens(gs_o, gs_t, 7)

    multiply(spec_s, spec_g, True, True)
    inner(wi_hi, wi_lo, z_buf, True)

    def store_filter(j, rows, lanes, y):
        gf_ref[pl.ds(rows, row_step), pl.ds(pl.multiple_of(j * tok + lanes, lane_step), lane_step)] = y

    inverse_outer(store_filter)

    hand_out(gf_ref, f_out, 4)

    wait_all(conv_o, 6)
    wait_all(gs_o, 7)
    for n, (src, dst) in enumerate(
        ((k_seq, k_out), (v_seq, v_out), (q_seq, q_out), (gtok, g_out), (gf_ref, f_out))
    ):
        pltpu.make_async_copy(src, dst, out_sem.at[n]).wait()

    def wait_sent(buf, n):
        pltpu.make_async_copy(buf, buf, send_sem.at[n]).wait()

    rows_sent = pl.ds(0, (n_ctx - 1) * slot)
    wait_sent(rk.at[rows_sent, :], 0)
    wait_sent(rv.at[rows_sent, :], 1)
    wait_sent(rq.at[rows_sent, :], 2)
    wait_sent(gtok.at[pl.ds(0, (n_tp - 1) * slot), :], 3)
    parts_sent = pl.ds(0, n_ctx - 1)
    wait_sent(sig_in.at[parts_sent], 4)
    wait_sent(gc_in.at[parts_sent], 5)
    wait_sent(conv_o.at[parts_sent], 6)
    wait_sent(gs_o.at[parts_sent], 7)


def finish_body(q, g, k, v, conv_t, gs_t, f_in, out, gq, gk, gv, f_out):
    conv = conv_t[...].astype(F32).T
    out[...] = (q[...].astype(F32) * conv).astype(BF)
    gq[...] = (g[...].astype(F32) * conv).astype(BF)
    grad = gs_t[...].astype(F32).T
    gk[...] = (grad * v[...].astype(F32)).astype(BF)
    gv[...] = (grad * k[...].astype(F32)).astype(BF)
    f_out[...] = f_in[...]


def finish(q, g, k, v, conv_t, gs_t, grad_filters):
    tok, width = q.shape
    chan, lags = grad_filters.shape
    steps = 4
    seq = pl.BlockSpec((tok, width // steps), lambda i: (0, i))
    seq_t = pl.BlockSpec((width // steps, tok), lambda i: (i, 0))
    filt = pl.BlockSpec((chan // steps, lags), lambda i: (i, 0))
    seq_out = jax.ShapeDtypeStruct((tok, width), BF)
    return pl.pallas_call(
        finish_body,
        grid=(steps,),
        out_shape=(seq_out,) * 4 + (jax.ShapeDtypeStruct((chan, lags), F32),),
        in_specs=[seq] * 4 + [seq_t] * 2 + [filt],
        out_specs=(seq,) * 4 + (filt,),
        compiler_params=pltpu.CompilerParams(vmem_limit_bytes=58 * 1024 * 1024),
    )(q, g, k, v, conv_t, gs_t, grad_filters)


def solution(mesh):
    n_ctx, n_tp = mesh.shape["ctx"], mesh.shape["tp"]

    def per_device(query_rows, key_rows, value_rows, positions, filters, bias_term, grad_out):
        width = query_rows.shape[1]
        slot = query_rows.shape[0] // n_ctx
        tok = grad_out.shape[0] * n_tp
        chan = filters.shape[0]
        (wf_hi, wf_lo), (wi_hi, wi_lo), cos, sin = make_tables(n_ctx, tok)
        own = lax.dynamic_slice_in_dim(positions, lax.axis_index("ctx") * slot, slot, 1)
        own = own.reshape(1, n_ctx * slot)
        bins = n_ctx + 1
        vm = pltpu.VMEM
        rows_bf = vm((n_ctx * slot, width), BF)
        seq = vm((tok, width), BF)
        seq_t = vm((width, tok), BF)
        parts = vm((n_ctx, chan, tok), BF)
        spec = vm((bins * chan, 2 * tok), F32)
        half_spec = vm((bins * chan, 2 * tok), BF)
        table = vm((2 * tok, 2 * tok), BF)
        any_spec = pl.BlockSpec(memory_space=pl.ANY)
        vmem_spec = pl.BlockSpec(memory_space=pltpu.VMEM)
        seq_out = jax.ShapeDtypeStruct((tok, width), BF)

        def body(*refs):
            kernel_body((n_ctx, n_tp, tok, slot, chan), *refs)

        seq_t_out = jax.ShapeDtypeStruct((width, tok), BF)

        parts_out = pl.pallas_call(
            body,
            out_shape=(seq_out,) * 4 + (seq_t_out,) * 2 + (jax.ShapeDtypeStruct(filters.shape, F32),),
            in_specs=[any_spec] * 9 + [vmem_spec] * 4,
            out_specs=(any_spec,) * 7,
            scratch_shapes=[
                rows_bf, rows_bf, rows_bf, seq, vm(filters.shape, F32), table, table, table, table,
                vm((tok, n_ctx * slot), BF), seq, seq, seq, seq_t, seq_t, parts, parts,
                half_spec, half_spec, spec, spec, spec, spec,
                parts, parts, vm(filters.shape, F32),
                pltpu.SemaphoreType.DMA((8,)),
                pltpu.SemaphoreType.DMA((8,)),
                pltpu.SemaphoreType.DMA((5,)),
                pltpu.SemaphoreType.DMA((5,)),
            ],
            compiler_params=pltpu.CompilerParams(
                collective_id=0, has_side_effects=True, vmem_limit_bytes=58 * 1024 * 1024
            ),
        )(
            query_rows, key_rows, value_rows, grad_out, filters,
            wf_hi, wf_lo, wi_hi, wi_lo,
            own, bias_term.reshape(chan, 1), cos, sin,
        )
        return finish(*parts_out)

    in_specs = (
        P("ctx", "tp"),
        P("ctx", "tp"),
        P("ctx", "tp"),
        P(),
        P(("tp", "ctx"), None),
        P(("tp", "ctx")),
        P(("ctx", "tp"), None),
    )
    out_specs = (
        P("ctx", "tp"),
        P("ctx", "tp"),
        P("ctx", "tp"),
        P("ctx", "tp"),
        P(("tp", "ctx"), None),
    )
    return jax.shard_map(
        per_device, mesh=mesh, in_specs=in_specs, out_specs=out_specs, check_vma=False
    )
```

```python
import math

import jax
import jax.numpy as jnp
import numpy as np
from jax import lax
from jax.experimental import pallas as pl
from jax.experimental.pallas import tpu as pltpu
from jax.sharding import PartitionSpec as P

MESH = pl.DeviceIdType.MESH
BF = jnp.bfloat16
F32 = jnp.float32
FAR_FIRST = (10, 5, 15, 13, 7, 14, 6, 11, 9, 2, 8, 1, 12, 3, 4)


def split_bf16(table):
    high = table.astype(jnp.bfloat16)
    low = (table - high.astype(np.float64)).astype(jnp.bfloat16)
    return high, low


def make_tables(shards, tokens):
    length = 2 * shards * tokens
    r = np.arange(tokens)
    inner = 2.0 * math.pi * ((r[:, None] * r[None, :]) % tokens) / tokens
    cos, sin = np.cos(inner), np.sin(inner)
    forward = np.block([[cos, -sin], [sin, cos]])
    backward = np.block([[cos, sin], [-sin, cos]])
    k = np.arange(shards + 1)
    twist = 2.0 * math.pi * (k[:, None] * r[None, :]) / length
    return (
        split_bf16(forward),
        split_bf16(backward),
        np.cos(twist).astype(np.float32),
        np.sin(twist).astype(np.float32),
    )


def real_dft_padded(xs):
    half = len(xs)
    if half == 1:
        return [(xs[0], None), (xs[0], None)]
    even = real_dft_padded(xs[0::2])
    odd = real_dft_padded(xs[1::2])
    out = [None] * (half + 1)
    out[0] = (even[0][0] + odd[0][0], None)
    out[half] = (even[0][0] - odd[0][0], None)
    mid = half // 2
    for k in range(1, mid):
        angle = math.pi * k / half
        c, s = math.cos(angle), math.sin(angle)
        o_re, o_im = odd[k]
        t_re = o_re * c + o_im * s
        t_im = o_im * c - o_re * s
        e_re, e_im = even[k]
        out[k] = (e_re + t_re, e_im + t_im)
        out[half - k] = (e_re - t_re, t_im - e_im)
    out[mid] = (even[mid][0], -odd[mid][0])
    return out


def real_inverse_half(bins):
    half = len(bins) - 1
    if half == 1:
        return [bins[0][0] + bins[1][0]]
    mid = half // 2
    even = [None] * (mid + 1)
    odd = [None] * (mid + 1)
    even[0] = (bins[0][0] + bins[half][0], None)
    odd[0] = (bins[0][0] - bins[half][0], None)
    for k in range(1, mid):
        angle = math.pi * k / half
        c, s = math.cos(angle), math.sin(angle)
        a_re, a_im = bins[k]
        b_re, b_im = bins[half - k]
        even[k] = (a_re + b_re, a_im - b_im)
        d_re, d_im = a_re - b_re, a_im + b_im
        odd[k] = (d_re * c - d_im * s, d_im * c + d_re * s)
    m_re, m_im = bins[mid]
    even[mid] = (m_re + m_re, None)
    odd[mid] = (-(m_im + m_im), None)
    y_even = real_inverse_half(even)
    y_odd = real_inverse_half(odd)
    out = [None] * half
    out[0::2] = y_even
    out[1::2] = y_odd
    return out


def kernel_body(
    sizes,
    q_hbm, k_hbm, v_hbm, g_hbm, f_hbm, wf_hi_hbm, wf_lo_hbm, wi_hi_hbm, wi_lo_hbm,
    positions_ref, bias_row, cos_ref, sin_ref,
    q_out, g_out, k_out, v_out, conv_t, gs_t, f_out,
    rq, rk, rv, gtok, f_buf, wf_hi, wf_lo, wi_hi, wi_lo,
    hot, q_seq, k_seq, v_seq, sig_t, gc_t, sig_in, gc_in,
    l_hi, l_lo, spec_f, spec_s, spec_g, z_buf,
    conv_o, gs_o, gf_ref, bias_ref,
    recv_sem, send_sem, local_sem, out_sem,
):
    n_ctx, n_tp, tok, slot, chan = sizes
    side = 4
    width = n_ctx * chan
    me = lax.axis_index("ctx")
    my_tp = lax.axis_index("tp")
    my_y, my_x = me // side, me % side
    factor = 1.0 / math.sqrt(n_ctx * tok)
    inv_len = 1.0 / (2 * n_ctx * tok)
    bins = n_ctx + 1

    def partner(o):
        return ((my_y + o // side) % side) * side + (my_x + o % side) % side

    def each_partner(fn):
        for o in FAR_FIRST:
            fn(partner(o))

    loads = [
        pltpu.make_async_copy(src, dst, local_sem.at[n])
        for n, (src, dst) in enumerate(
            ((f_hbm, f_buf), (wf_hi_hbm, wf_hi), (wf_lo_hbm, wf_lo), (wi_hi_hbm, wi_hi), (wi_lo_hbm, wi_lo))
        )
    ]
    for copy in loads:
        copy.start()

    barrier = pltpu.get_barrier_semaphore()
    each_partner(
        lambda d: pl.semaphore_signal(barrier, inc=1, device_id=(d, my_tp), device_id_type=MESH)
    )
    lax.fori_loop(
        1,
        n_tp,
        lambda o, c: (
            pl.semaphore_signal(
                barrier, inc=1, device_id=(me, (my_tp + o) % n_tp), device_id_type=MESH
            ),
            c,
        )[1],
        0,
    )
    pl.semaphore_wait(barrier, n_ctx + n_tp - 2)

    def send_rows(src, dst, n):
        def one(d):
            pltpu.make_async_remote_copy(
                src_ref=src.at[pl.ds(pl.multiple_of(d * slot, slot), slot), :],
                dst_ref=dst.at[pl.ds(pl.multiple_of(me * slot, slot), slot), :],
                send_sem=send_sem.at[n],
                recv_sem=recv_sem.at[n],
                device_id=(d, my_tp),
                device_id_type=MESH,
            ).start()

        own = pl.ds(pl.multiple_of(me * slot, slot), slot)
        pltpu.make_async_copy(src.at[own, :], dst.at[own, :], recv_sem.at[n]).start()
        each_partner(one)

    send_rows(k_hbm, rk, 0)
    send_rows(v_hbm, rv, 1)

    def send_grad(o, carry):
        d = (my_tp + o) % n_tp
        pltpu.make_async_remote_copy(
            src_ref=g_hbm.at[:, pl.ds(pl.multiple_of(d * width, width), width)],
            dst_ref=gtok.at[pl.ds(pl.multiple_of(my_tp * slot, slot), slot), :],
            send_sem=send_sem.at[3],
            recv_sem=recv_sem.at[3],
            device_id=(me, d),
            device_id_type=MESH,
        ).start()
        return carry

    pltpu.make_async_copy(
        g_hbm.at[:, pl.ds(pl.multiple_of(my_tp * width, width), width)],
        gtok.at[pl.ds(pl.multiple_of(my_tp * slot, slot), slot), :],
        recv_sem.at[3],
    ).start()
    lax.fori_loop(1, n_tp, send_grad, 0)
    send_rows(q_hbm, rq, 2)

    rows_all = n_ctx * slot
    lane = lax.broadcasted_iota(jnp.int32, (rows_all, rows_all), 1)
    column = lax.broadcasted_iota(jnp.int32, (rows_all, rows_all), 0)
    pick = jnp.where(column == me * slot + lane % slot, 1.0, 0.0).astype(BF)
    mine = jnp.dot(
        positions_ref[...].astype(F32).astype(BF), pick, preferred_element_type=F32
    )
    buffer = lax.broadcasted_iota(jnp.int32, mine.shape, 0)
    keep = lax.broadcasted_iota(jnp.int32, mine.shape, 1) // slot == buffer
    slots = jnp.sum(jnp.where(keep, mine, 0.0), axis=0, keepdims=True).astype(jnp.int32)
    bias_ref[...] = jnp.broadcast_to(bias_row[...], (128, chan)).T
    hot[...] = jnp.where(
        slots == lax.broadcasted_iota(jnp.int32, hot.shape, 0), 1.0, 0.0
    ).astype(BF)

    row_step, lane_step = 16, 128
    halves = tok // lane_step
    pieces = (chan // row_step) * halves

    def place(it):
        rows = pl.multiple_of((it // halves) * row_step, row_step)
        lanes = pl.multiple_of((it % halves) * lane_step, lane_step)
        return rows, lanes

    def put_split(row, lane, value, exact):
        high = value.astype(BF)
        at = (pl.ds(pl.multiple_of(row, row_step), row_step), pl.ds(pl.multiple_of(lane, lane_step), lane_step))
        l_hi[at] = high
        if exact:
            l_lo[at] = (value - high.astype(F32)).astype(BF)

    def forward_outer(load, exact):
        def step(it, carry):
            rows, lanes = place(it)
            spectrum = real_dft_padded([load(j, rows, lanes) for j in range(n_ctx)])
            for k in range(bins):
                re, im = spectrum[k]
                if k == 0:
                    put_split(rows, lanes, re, exact)
                    put_split(rows, tok + lanes, jnp.zeros_like(re), exact)
                    continue
                c = cos_ref[k : k + 1, pl.ds(lanes, lane_step)]
                s = sin_ref[k : k + 1, pl.ds(lanes, lane_step)]
                if im is None:
                    t_re, t_im = re * c, -(re * s)
                else:
                    t_re, t_im = re * c + im * s, im * c - re * s
                put_split(k * chan + rows, lanes, t_re, exact)
                put_split(k * chan + rows, tok + lanes, t_im, exact)
            return carry

        lax.fori_loop(0, pieces, step, 0)

    total_rows = bins * chan
    block_rows = total_rows // 4

    def inner(high, low, dest, exact):
        def step(m, carry):
            at = pl.ds(pl.multiple_of(m * block_rows, row_step), block_rows)
            a = l_hi[at, :]
            total = jnp.dot(a, high[...], preferred_element_type=F32)
            if exact:
                total += jnp.dot(a, low[...], preferred_element_type=F32)
                total += jnp.dot(l_lo[at, :], high[...], preferred_element_type=F32)
            dest[at, :] = total
            return carry

        lax.fori_loop(0, 4, step, 0)

    def multiply(one, two, conjugate_one, exact):
        def step(m, carry):
            row = m * row_step
            at = pl.ds(pl.multiple_of(row, row_step), row_step)
            for lane in range(0, tok, lane_step):
                re_at, im_at = slice(lane, lane + lane_step), slice(tok + lane, tok + lane + lane_step)
                a, b = one[at, re_at], one[at, im_at]
                c, d = two[at, re_at], two[at, im_at]
                if conjugate_one:
                    re, im = a * c + b * d, a * d - b * c
                else:
                    re, im = a * c - b * d, a * d + b * c
                put_split(row, lane, re, exact)
                put_split(row, tok + lane, im, exact)
            return carry

        lax.fori_loop(0, total_rows // row_step, step, 0)

    def inverse_outer(store):
        def step(it, carry):
            rows, lanes = place(it)
            spectrum = []
            for k in range(bins):
                at = pl.ds(pl.multiple_of(k * chan + rows, row_step), row_step)
                re = z_buf[at, pl.ds(lanes, lane_step)]
                if k == 0:
                    spectrum.append((re, None))
                    continue
                im = z_buf[at, pl.ds(pl.multiple_of(tok + lanes, lane_step), lane_step)]
                c = cos_ref[k : k + 1, pl.ds(lanes, lane_step)]
                s = sin_ref[k : k + 1, pl.ds(lanes, lane_step)]
                if k == n_ctx:
                    spectrum.append((re * c - im * s, None))
                else:
                    spectrum.append((re * c - im * s, im * c + re * s))
            for j, y in enumerate(real_inverse_half(spectrum)):
                store(j, rows, lanes, y * (factor * inv_len))
            return carry

        lax.fori_loop(0, pieces, step, 0)

    for copy in loads:
        copy.wait()
    forward_outer(
        lambda j, rows, lanes: f_buf[
            pl.ds(rows, row_step), pl.ds(pl.multiple_of(j * tok + lanes, lane_step), lane_step)
        ],
        True,
    )
    inner(wf_hi, wf_lo, spec_f, True)

    def wait_all(buf, n):
        pltpu.make_async_copy(buf, buf, recv_sem.at[n]).wait()

    def hand_out(src, dst, n):
        pltpu.make_async_copy(src, dst, out_sem.at[n]).start()

    def settled(rows_ref, cols):
        return jnp.dot(hot[...], rows_ref[:, cols], preferred_element_type=F32)

    group = side * chan

    def send_channels(src, dst, n, y):
        for dx in (2, 1, 3, 0):
            d = y * side + (my_x + dx) % side
            at = pl.ds(pl.multiple_of(d * chan, chan), chan)
            pl.when(d != me)(
                lambda: pltpu.make_async_remote_copy(
                    src_ref=src.at[at, :],
                    dst_ref=dst.at[me],
                    send_sem=send_sem.at[n],
                    recv_sem=recv_sem.at[n],
                    device_id=(d, my_tp),
                    device_id_type=MESH,
                ).start()
            )

    def send_own_channels(src, dst, n):
        at = pl.ds(pl.multiple_of(me * chan, chan), chan)
        pltpu.make_async_copy(src.at[at, :], dst.at[me], recv_sem.at[n]).start()

    wait_all(rk, 0)
    wait_all(rv, 1)

    def signal_step(i, carry):
        y = (my_y + i + 1) % side
        cols = pl.ds(pl.multiple_of(y * group, group), group)
        key = settled(rk, cols)
        value = settled(rv, cols)
        k_seq[:, cols] = key.astype(BF)
        v_seq[:, cols] = value.astype(BF)
        sig_t[cols, :] = (key * value).T.astype(BF)
        send_channels(sig_t, sig_in, 4, y)
        return carry

    lax.fori_loop(0, side, signal_step, 0)
    send_own_channels(sig_t, sig_in, 4)
    hand_out(k_seq, k_out, 0)
    hand_out(v_seq, v_out, 1)

    wait_all(rq, 2)
    wait_all(gtok, 3)

    def grad_step(i, carry):
        y = (my_y + i + 1) % side
        cols = pl.ds(pl.multiple_of(y * group, group), group)
        query = settled(rq, cols)
        q_seq[:, cols] = query.astype(BF)
        gc_t[cols, :] = (query * gtok[:, cols].astype(F32)).T.astype(BF)
        send_channels(gc_t, gc_in, 5, y)
        return carry

    lax.fori_loop(0, side, grad_step, 0)
    send_own_channels(gc_t, gc_in, 5)
    hand_out(q_seq, q_out, 2)
    hand_out(gtok, g_out, 3)

    def send_tokens(src, dst, n):
        at = pl.ds(pl.multiple_of(me * chan, chan), chan)

        def one(d):
            pltpu.make_async_remote_copy(
                src_ref=src.at[d],
                dst_ref=dst.at[at, :],
                send_sem=send_sem.at[n],
                recv_sem=recv_sem.at[n],
                device_id=(d, my_tp),
                device_id_type=MESH,
            ).start()

        pltpu.make_async_copy(src.at[me], dst.at[at, :], recv_sem.at[n]).start()
        each_partner(one)

    def piece(buf, j, rows, lanes):
        return buf[j, pl.ds(rows, row_step), pl.ds(lanes, lane_step)].astype(F32)

    def store_with_bias(direct, dest):
        def store(j, rows, lanes, y):
            bias = bias_ref[pl.ds(rows, row_step), :]
            dest[j, pl.ds(rows, row_step), pl.ds(lanes, lane_step)] = (
                bias * piece(direct, j, rows, lanes) + y
            ).astype(BF)

        return store

    wait_all(sig_in, 4)
    forward_outer(lambda j, rows, lanes: piece(sig_in, j, rows, lanes), False)
    inner(wf_hi, wf_lo, spec_s, False)
    multiply(spec_f, spec_s, False, False)
    inner(wi_hi, wi_lo, z_buf, False)
    inverse_outer(store_with_bias(sig_in, conv_o))
    send_tokens(conv_o, conv_t, 6)

    wait_all(gc_in, 5)
    forward_outer(lambda j, rows, lanes: piece(gc_in, j, rows, lanes), False)
    inner(wf_hi, wf_lo, spec_g, False)
    multiply(spec_f, spec_g, True, False)
    inner(wi_hi, wi_lo, z_buf, False)
    inverse_outer(store_with_bias(gc_in, gs_o))
    send_tokens(gs_o, gs_t, 7)

    multiply(spec_s, spec_g, True, True)
    inner(wi_hi, wi_lo, z_buf, True)

    def store_filter(j, rows, lanes, y):
        gf_ref[pl.ds(rows, row_step), pl.ds(pl.multiple_of(j * tok + lanes, lane_step), lane_step)] = y

    inverse_outer(store_filter)

    hand_out(gf_ref, f_out, 4)

    wait_all(conv_o, 6)
    wait_all(gs_o, 7)
    for n, (src, dst) in enumerate(
        ((k_seq, k_out), (v_seq, v_out), (q_seq, q_out), (gtok, g_out), (gf_ref, f_out))
    ):
        pltpu.make_async_copy(src, dst, out_sem.at[n]).wait()

    def wait_sent(buf, n):
        pltpu.make_async_copy(buf, buf, send_sem.at[n]).wait()

    rows_sent = pl.ds(0, (n_ctx - 1) * slot)
    wait_sent(rk.at[rows_sent, :], 0)
    wait_sent(rv.at[rows_sent, :], 1)
    wait_sent(rq.at[rows_sent, :], 2)
    wait_sent(gtok.at[pl.ds(0, (n_tp - 1) * slot), :], 3)
    parts_sent = pl.ds(0, n_ctx - 1)
    wait_sent(sig_in.at[parts_sent], 4)
    wait_sent(gc_in.at[parts_sent], 5)
    wait_sent(conv_o.at[parts_sent], 6)
    wait_sent(gs_o.at[parts_sent], 7)


def finish_body(q, g, k, v, conv_t, gs_t, f_in, out, gq, gk, gv, f_out):
    conv = conv_t[...].astype(F32).T
    out[...] = (q[...].astype(F32) * conv).astype(BF)
    gq[...] = (g[...].astype(F32) * conv).astype(BF)
    grad = gs_t[...].astype(F32).T
    gk[...] = (grad * v[...].astype(F32)).astype(BF)
    gv[...] = (grad * k[...].astype(F32)).astype(BF)
    f_out[...] = f_in[...]


def finish(q, g, k, v, conv_t, gs_t, grad_filters):
    tok, width = q.shape
    chan, lags = grad_filters.shape
    steps = 4
    seq = pl.BlockSpec((tok, width // steps), lambda i: (0, i))
    seq_t = pl.BlockSpec((width // steps, tok), lambda i: (i, 0))
    filt = pl.BlockSpec((chan // steps, lags), lambda i: (i, 0))
    seq_out = jax.ShapeDtypeStruct((tok, width), BF)
    return pl.pallas_call(
        finish_body,
        grid=(steps,),
        out_shape=(seq_out,) * 4 + (jax.ShapeDtypeStruct((chan, lags), F32),),
        in_specs=[seq] * 4 + [seq_t] * 2 + [filt],
        out_specs=(seq,) * 4 + (filt,),
        compiler_params=pltpu.CompilerParams(vmem_limit_bytes=58 * 1024 * 1024),
    )(q, g, k, v, conv_t, gs_t, grad_filters)


def solution(mesh):
    n_ctx, n_tp = mesh.shape["ctx"], mesh.shape["tp"]

    def per_device(query_rows, key_rows, value_rows, positions, filters, bias_term, grad_out):
        width = query_rows.shape[1]
        slot = query_rows.shape[0] // n_ctx
        tok = grad_out.shape[0] * n_tp
        chan = filters.shape[0]
        (wf_hi, wf_lo), (wi_hi, wi_lo), cos, sin = make_tables(n_ctx, tok)
        bins = n_ctx + 1
        vm = pltpu.VMEM
        rows_bf = vm((n_ctx * slot, width), BF)
        seq = vm((tok, width), BF)
        seq_t = vm((width, tok), BF)
        parts = vm((n_ctx, chan, tok), BF)
        spec = vm((bins * chan, 2 * tok), F32)
        half_spec = vm((bins * chan, 2 * tok), BF)
        table = vm((2 * tok, 2 * tok), BF)
        any_spec = pl.BlockSpec(memory_space=pl.ANY)
        vmem_spec = pl.BlockSpec(memory_space=pltpu.VMEM)
        seq_out = jax.ShapeDtypeStruct((tok, width), BF)

        def body(*refs):
            kernel_body((n_ctx, n_tp, tok, slot, chan), *refs)

        seq_t_out = jax.ShapeDtypeStruct((width, tok), BF)

        parts_out = pl.pallas_call(
            body,
            out_shape=(seq_out,) * 4 + (seq_t_out,) * 2 + (jax.ShapeDtypeStruct(filters.shape, F32),),
            in_specs=[any_spec] * 9 + [vmem_spec] * 4,
            out_specs=(any_spec,) * 7,
            scratch_shapes=[
                rows_bf, rows_bf, rows_bf, seq, vm(filters.shape, F32), table, table, table, table,
                vm((tok, n_ctx * slot), BF), seq, seq, seq, seq_t, seq_t, parts, parts,
                half_spec, half_spec, spec, spec, spec, spec,
                parts, parts, vm(filters.shape, F32), vm((chan, 128), F32),
                pltpu.SemaphoreType.DMA((8,)),
                pltpu.SemaphoreType.DMA((8,)),
                pltpu.SemaphoreType.DMA((5,)),
                pltpu.SemaphoreType.DMA((5,)),
            ],
            compiler_params=pltpu.CompilerParams(
                collective_id=0, has_side_effects=True, vmem_limit_bytes=58 * 1024 * 1024
            ),
        )(
            query_rows, key_rows, value_rows, grad_out, filters,
            wf_hi, wf_lo, wi_hi, wi_lo,
            positions, bias_term.reshape(1, chan), cos, sin,
        )
        return finish(*parts_out)

    in_specs = (
        P("ctx", "tp"),
        P("ctx", "tp"),
        P("ctx", "tp"),
        P(),
        P(("tp", "ctx"), None),
        P(("tp", "ctx")),
        P(("ctx", "tp"), None),
    )
    out_specs = (
        P("ctx", "tp"),
        P("ctx", "tp"),
        P("ctx", "tp"),
        P("ctx", "tp"),
        P(("tp", "ctx"), None),
    )
    return jax.shard_map(
        per_device, mesh=mesh, in_specs=in_specs, out_specs=out_specs, check_vma=False
    )
```

```python
import math

import jax
import jax.numpy as jnp
import numpy as np
from jax import lax
from jax.experimental import pallas as pl
from jax.experimental.pallas import tpu as pltpu
from jax.sharding import PartitionSpec as P

MESH = pl.DeviceIdType.MESH
BF = jnp.bfloat16
F32 = jnp.float32
FAR_FIRST = (10, 5, 15, 13, 7, 14, 6, 11, 9, 2, 8, 1, 12, 3, 4)


def split_bf16(table):
    high = table.astype(jnp.bfloat16)
    low = (table - high.astype(np.float64)).astype(jnp.bfloat16)
    return high, low


def make_tables(shards, tokens):
    length = 2 * shards * tokens
    r = np.arange(tokens)
    inner = 2.0 * math.pi * ((r[:, None] * r[None, :]) % tokens) / tokens
    cos, sin = np.cos(inner), np.sin(inner)
    forward = np.block([[cos, -sin], [sin, cos]])
    backward = np.block([[cos, sin], [-sin, cos]])
    k = np.arange(shards + 1)
    twist = 2.0 * math.pi * (k[:, None] * r[None, :]) / length
    return (
        split_bf16(forward),
        split_bf16(backward),
        np.cos(twist).astype(np.float32),
        np.sin(twist).astype(np.float32),
    )


def real_dft_padded(xs):
    half = len(xs)
    if half == 1:
        return [(xs[0], None), (xs[0], None)]
    even = real_dft_padded(xs[0::2])
    odd = real_dft_padded(xs[1::2])
    out = [None] * (half + 1)
    out[0] = (even[0][0] + odd[0][0], None)
    out[half] = (even[0][0] - odd[0][0], None)
    mid = half // 2
    for k in range(1, mid):
        angle = math.pi * k / half
        c, s = math.cos(angle), math.sin(angle)
        o_re, o_im = odd[k]
        t_re = o_re * c + o_im * s
        t_im = o_im * c - o_re * s
        e_re, e_im = even[k]
        out[k] = (e_re + t_re, e_im + t_im)
        out[half - k] = (e_re - t_re, t_im - e_im)
    out[mid] = (even[mid][0], -odd[mid][0])
    return out


def real_inverse_half(bins):
    half = len(bins) - 1
    if half == 1:
        return [bins[0][0] + bins[1][0]]
    mid = half // 2
    even = [None] * (mid + 1)
    odd = [None] * (mid + 1)
    even[0] = (bins[0][0] + bins[half][0], None)
    odd[0] = (bins[0][0] - bins[half][0], None)
    for k in range(1, mid):
        angle = math.pi * k / half
        c, s = math.cos(angle), math.sin(angle)
        a_re, a_im = bins[k]
        b_re, b_im = bins[half - k]
        even[k] = (a_re + b_re, a_im - b_im)
        d_re, d_im = a_re - b_re, a_im + b_im
        odd[k] = (d_re * c - d_im * s, d_im * c + d_re * s)
    m_re, m_im = bins[mid]
    even[mid] = (m_re + m_re, None)
    odd[mid] = (-(m_im + m_im), None)
    y_even = real_inverse_half(even)
    y_odd = real_inverse_half(odd)
    out = [None] * half
    out[0::2] = y_even
    out[1::2] = y_odd
    return out


def kernel_body(
    sizes,
    q_hbm, k_hbm, v_hbm, g_hbm, f_hbm, wf_hi_hbm, wf_lo_hbm, wi_hi_hbm, wi_lo_hbm,
    positions_ref, bias_row, cos_ref, sin_ref,
    q_out, g_out, k_out, v_out, conv_t, gs_t, f_out,
    rq, rk, rv, gtok, f_buf, wf_hi, wf_lo, wi_hi, wi_lo,
    hot, q_seq, k_seq, v_seq, sig_t, gc_t, sig_in, gc_in,
    l_hi, l_lo, spec_f, spec_s, spec_g, z_buf,
    conv_o, gs_o, gf_ref, bias_ref,
    recv_sem, send_sem, local_sem, out_sem,
):
    n_ctx, n_tp, tok, slot, chan = sizes
    side = 4
    width = n_ctx * chan
    me = lax.axis_index("ctx")
    my_tp = lax.axis_index("tp")
    my_y, my_x = me // side, me % side
    factor = 1.0 / math.sqrt(n_ctx * tok)
    inv_len = 1.0 / (2 * n_ctx * tok)
    bins = n_ctx + 1

    def partner(o):
        return ((my_y + o // side) % side) * side + (my_x + o % side) % side

    def each_partner(fn):
        for o in FAR_FIRST:
            fn(partner(o))

    loads = [
        pltpu.make_async_copy(src, dst, local_sem.at[n])
        for n, (src, dst) in enumerate(
            ((f_hbm, f_buf), (wf_hi_hbm, wf_hi), (wf_lo_hbm, wf_lo), (wi_hi_hbm, wi_hi), (wi_lo_hbm, wi_lo))
        )
    ]
    for copy in loads:
        copy.start()

    barrier = pltpu.get_barrier_semaphore()
    each_partner(
        lambda d: pl.semaphore_signal(barrier, inc=1, device_id=(d, my_tp), device_id_type=MESH)
    )
    lax.fori_loop(
        1,
        n_tp,
        lambda o, c: (
            pl.semaphore_signal(
                barrier, inc=1, device_id=(me, (my_tp + o) % n_tp), device_id_type=MESH
            ),
            c,
        )[1],
        0,
    )
    pl.semaphore_wait(barrier, n_ctx + n_tp - 2)

    def send_rows(src, dst, n):
        def one(d):
            pltpu.make_async_remote_copy(
                src_ref=src.at[pl.ds(pl.multiple_of(d * slot, slot), slot), :],
                dst_ref=dst.at[pl.ds(pl.multiple_of(me * slot, slot), slot), :],
                send_sem=send_sem.at[n],
                recv_sem=recv_sem.at[n],
                device_id=(d, my_tp),
                device_id_type=MESH,
            ).start()

        own = pl.ds(pl.multiple_of(me * slot, slot), slot)
        pltpu.make_async_copy(src.at[own, :], dst.at[own, :], recv_sem.at[n]).start()
        each_partner(one)

    send_rows(k_hbm, rk, 0)
    send_rows(v_hbm, rv, 1)

    def send_grad(o, carry):
        d = (my_tp + o) % n_tp
        pltpu.make_async_remote_copy(
            src_ref=g_hbm.at[:, pl.ds(pl.multiple_of(d * width, width), width)],
            dst_ref=gtok.at[pl.ds(pl.multiple_of(my_tp * slot, slot), slot), :],
            send_sem=send_sem.at[3],
            recv_sem=recv_sem.at[3],
            device_id=(me, d),
            device_id_type=MESH,
        ).start()
        return carry

    pltpu.make_async_copy(
        g_hbm.at[:, pl.ds(pl.multiple_of(my_tp * width, width), width)],
        gtok.at[pl.ds(pl.multiple_of(my_tp * slot, slot), slot), :],
        recv_sem.at[3],
    ).start()
    lax.fori_loop(1, n_tp, send_grad, 0)
    send_rows(q_hbm, rq, 2)

    rows_all = n_ctx * slot
    lane = lax.broadcasted_iota(jnp.int32, (rows_all, rows_all), 1)
    column = lax.broadcasted_iota(jnp.int32, (rows_all, rows_all), 0)
    pick = jnp.where(column == me * slot + lane % slot, 1.0, 0.0).astype(BF)
    mine = jnp.dot(
        positions_ref[...].astype(F32).astype(BF), pick, preferred_element_type=F32
    )
    buffer = lax.broadcasted_iota(jnp.int32, mine.shape, 0)
    keep = lax.broadcasted_iota(jnp.int32, mine.shape, 1) // slot == buffer
    slots = jnp.sum(jnp.where(keep, mine, 0.0), axis=0, keepdims=True).astype(jnp.int32)
    bias_ref[...] = jnp.broadcast_to(bias_row[...], (128, chan)).T
    hot[...] = jnp.where(
        slots == lax.broadcasted_iota(jnp.int32, hot.shape, 0), 1.0, 0.0
    ).astype(BF)

    row_step, lane_step = 16, 128
    halves = tok // lane_step
    pieces = (chan // row_step) * halves

    def place(it):
        rows = pl.multiple_of((it // halves) * row_step, row_step)
        lanes = pl.multiple_of((it % halves) * lane_step, lane_step)
        return rows, lanes

    def put_split(row, lane, value, exact):
        high = value.astype(BF)
        at = (pl.ds(pl.multiple_of(row, row_step), row_step), pl.ds(pl.multiple_of(lane, lane_step), lane_step))
        l_hi[at] = high
        if exact:
            l_lo[at] = (value - high.astype(F32)).astype(BF)

    def forward_outer(load, exact):
        def step(it, carry):
            rows, lanes = place(it)
            spectrum = real_dft_padded([load(j, rows, lanes) for j in range(n_ctx)])
            for k in range(bins):
                re, im = spectrum[k]
                if k == 0:
                    put_split(rows, lanes, re, exact)
                    put_split(rows, tok + lanes, jnp.zeros_like(re), exact)
                    continue
                c = cos_ref[k : k + 1, pl.ds(lanes, lane_step)]
                s = sin_ref[k : k + 1, pl.ds(lanes, lane_step)]
                if im is None:
                    t_re, t_im = re * c, -(re * s)
                else:
                    t_re, t_im = re * c + im * s, im * c - re * s
                put_split(k * chan + rows, lanes, t_re, exact)
                put_split(k * chan + rows, tok + lanes, t_im, exact)
            return carry

        lax.fori_loop(0, pieces, step, 0)

    total_rows = bins * chan
    block_rows = total_rows // 4

    def inner(high, low, dest, exact):
        def step(m, carry):
            at = pl.ds(pl.multiple_of(m * block_rows, row_step), block_rows)
            a = l_hi[at, :]
            total = jnp.dot(a, high[...], preferred_element_type=F32)
            if exact:
                total += jnp.dot(a, low[...], preferred_element_type=F32)
                total += jnp.dot(l_lo[at, :], high[...], preferred_element_type=F32)
            dest[at, :] = total
            return carry

        lax.fori_loop(0, 4, step, 0)

    def multiply(one, two, conjugate_one, exact):
        def step(m, carry):
            row = m * row_step
            at = pl.ds(pl.multiple_of(row, row_step), row_step)
            for lane in range(0, tok, lane_step):
                re_at, im_at = slice(lane, lane + lane_step), slice(tok + lane, tok + lane + lane_step)
                a, b = one[at, re_at], one[at, im_at]
                c, d = two[at, re_at], two[at, im_at]
                if conjugate_one:
                    re, im = a * c + b * d, a * d - b * c
                else:
                    re, im = a * c - b * d, a * d + b * c
                put_split(row, lane, re, exact)
                put_split(row, tok + lane, im, exact)
            return carry

        lax.fori_loop(0, total_rows // row_step, step, 0)

    def inverse_outer(store, middle=None):
        def step(it, carry):
            rows, lanes = place(it)
            spectrum = []
            for k in range(bins):
                at = pl.ds(pl.multiple_of(k * chan + rows, row_step), row_step)
                re = z_buf[at, pl.ds(lanes, lane_step)]
                if k == 0:
                    spectrum.append((re, None))
                    continue
                im = z_buf[at, pl.ds(pl.multiple_of(tok + lanes, lane_step), lane_step)]
                c = cos_ref[k : k + 1, pl.ds(lanes, lane_step)]
                s = sin_ref[k : k + 1, pl.ds(lanes, lane_step)]
                if k == n_ctx:
                    spectrum.append((re * c - im * s, None))
                else:
                    spectrum.append((re * c - im * s, im * c + re * s))
            for j, y in enumerate(real_inverse_half(spectrum)):
                store(j, rows, lanes, y * (factor * inv_len))
            return carry

        lax.fori_loop(0, pieces // 2, step, 0)
        if middle is not None:
            middle()
        lax.fori_loop(pieces // 2, pieces, step, 0)

    for copy in loads:
        copy.wait()
    forward_outer(
        lambda j, rows, lanes: f_buf[
            pl.ds(rows, row_step), pl.ds(pl.multiple_of(j * tok + lanes, lane_step), lane_step)
        ],
        True,
    )
    inner(wf_hi, wf_lo, spec_f, True)

    def wait_all(buf, n):
        pltpu.make_async_copy(buf, buf, recv_sem.at[n]).wait()

    def hand_out(src, dst, n):
        pltpu.make_async_copy(src, dst, out_sem.at[n]).start()

    def settled(rows_ref, cols):
        return jnp.dot(hot[...], rows_ref[:, cols], preferred_element_type=F32)

    group = side * chan

    def send_channels(src, dst, n, y):
        for dx in (2, 1, 3, 0):
            d = y * side + (my_x + dx) % side
            at = pl.ds(pl.multiple_of(d * chan, chan), chan)
            pl.when(d != me)(
                lambda: pltpu.make_async_remote_copy(
                    src_ref=src.at[at, :],
                    dst_ref=dst.at[me],
                    send_sem=send_sem.at[n],
                    recv_sem=recv_sem.at[n],
                    device_id=(d, my_tp),
                    device_id_type=MESH,
                ).start()
            )

    def send_own_channels(src, dst, n):
        at = pl.ds(pl.multiple_of(me * chan, chan), chan)
        pltpu.make_async_copy(src.at[at, :], dst.at[me], recv_sem.at[n]).start()

    wait_all(rk, 0)
    wait_all(rv, 1)

    def signal_step(i, carry):
        y = (my_y + i + 1) % side
        cols = pl.ds(pl.multiple_of(y * group, group), group)
        key = settled(rk, cols)
        value = settled(rv, cols)
        k_seq[:, cols] = key.astype(BF)
        v_seq[:, cols] = value.astype(BF)
        sig_t[cols, :] = (key * value).T.astype(BF)
        send_channels(sig_t, sig_in, 4, y)
        return carry

    lax.fori_loop(0, side, signal_step, 0)
    send_own_channels(sig_t, sig_in, 4)
    hand_out(k_seq, k_out, 0)
    hand_out(v_seq, v_out, 1)

    wait_all(rq, 2)
    wait_all(gtok, 3)

    def grad_step(i, carry):
        y = (my_y + i + 1) % side
        cols = pl.ds(pl.multiple_of(y * group, group), group)
        query = settled(rq, cols)
        q_seq[:, cols] = query.astype(BF)
        gc_t[cols, :] = (query * gtok[:, cols].astype(F32)).T.astype(BF)
        send_channels(gc_t, gc_in, 5, y)
        return carry

    lax.fori_loop(0, side, grad_step, 0)
    send_own_channels(gc_t, gc_in, 5)
    hand_out(q_seq, q_out, 2)
    hand_out(gtok, g_out, 3)

    half_chan = chan // 2

    def send_tokens(src, dst, n, part):
        from_rows = pl.ds(part * half_chan, half_chan)
        at = pl.ds(pl.multiple_of(me * chan + part * half_chan, half_chan), half_chan)

        def one(d):
            pltpu.make_async_remote_copy(
                src_ref=src.at[d, from_rows, :],
                dst_ref=dst.at[at, :],
                send_sem=send_sem.at[n],
                recv_sem=recv_sem.at[n],
                device_id=(d, my_tp),
                device_id_type=MESH,
            ).start()

        pltpu.make_async_copy(src.at[me, from_rows, :], dst.at[at, :], recv_sem.at[n]).start()
        each_partner(one)

    def piece(buf, j, rows, lanes):
        return buf[j, pl.ds(rows, row_step), pl.ds(lanes, lane_step)].astype(F32)

    def store_with_bias(direct, dest):
        def store(j, rows, lanes, y):
            bias = bias_ref[pl.ds(rows, row_step), :]
            dest[j, pl.ds(rows, row_step), pl.ds(lanes, lane_step)] = (
                bias * piece(direct, j, rows, lanes) + y
            ).astype(BF)

        return store

    wait_all(sig_in, 4)
    forward_outer(lambda j, rows, lanes: piece(sig_in, j, rows, lanes), False)
    inner(wf_hi, wf_lo, spec_s, False)
    multiply(spec_f, spec_s, False, False)
    inner(wi_hi, wi_lo, z_buf, False)
    inverse_outer(store_with_bias(sig_in, conv_o), lambda: send_tokens(conv_o, conv_t, 6, 0))
    send_tokens(conv_o, conv_t, 6, 1)

    wait_all(gc_in, 5)
    forward_outer(lambda j, rows, lanes: piece(gc_in, j, rows, lanes), False)
    inner(wf_hi, wf_lo, spec_g, False)
    multiply(spec_f, spec_g, True, False)
    inner(wi_hi, wi_lo, z_buf, False)
    inverse_outer(store_with_bias(gc_in, gs_o), lambda: send_tokens(gs_o, gs_t, 7, 0))
    send_tokens(gs_o, gs_t, 7, 1)

    multiply(spec_s, spec_g, True, True)
    inner(wi_hi, wi_lo, z_buf, True)

    def store_filter(j, rows, lanes, y):
        gf_ref[pl.ds(rows, row_step), pl.ds(pl.multiple_of(j * tok + lanes, lane_step), lane_step)] = y

    inverse_outer(store_filter)

    hand_out(gf_ref, f_out, 4)

    wait_all(conv_o, 6)
    wait_all(gs_o, 7)
    for n, (src, dst) in enumerate(
        ((k_seq, k_out), (v_seq, v_out), (q_seq, q_out), (gtok, g_out), (gf_ref, f_out))
    ):
        pltpu.make_async_copy(src, dst, out_sem.at[n]).wait()

    def wait_sent(buf, n):
        pltpu.make_async_copy(buf, buf, send_sem.at[n]).wait()

    rows_sent = pl.ds(0, (n_ctx - 1) * slot)
    wait_sent(rk.at[rows_sent, :], 0)
    wait_sent(rv.at[rows_sent, :], 1)
    wait_sent(rq.at[rows_sent, :], 2)
    wait_sent(gtok.at[pl.ds(0, (n_tp - 1) * slot), :], 3)
    parts_sent = pl.ds(0, n_ctx - 1)
    wait_sent(sig_in.at[parts_sent], 4)
    wait_sent(gc_in.at[parts_sent], 5)
    wait_sent(conv_o.at[parts_sent], 6)
    wait_sent(gs_o.at[parts_sent], 7)


def finish_body(q, g, k, v, conv_t, gs_t, f_in, out, gq, gk, gv, f_out):
    conv = conv_t[...].astype(F32).T
    out[...] = (q[...].astype(F32) * conv).astype(BF)
    gq[...] = (g[...].astype(F32) * conv).astype(BF)
    grad = gs_t[...].astype(F32).T
    gk[...] = (grad * v[...].astype(F32)).astype(BF)
    gv[...] = (grad * k[...].astype(F32)).astype(BF)
    f_out[...] = f_in[...]


def finish(q, g, k, v, conv_t, gs_t, grad_filters):
    tok, width = q.shape
    chan, lags = grad_filters.shape
    steps = 2
    seq = pl.BlockSpec((tok, width // steps), lambda i: (0, i))
    seq_t = pl.BlockSpec((width // steps, tok), lambda i: (i, 0))
    filt = pl.BlockSpec((chan // steps, lags), lambda i: (i, 0))
    seq_out = jax.ShapeDtypeStruct((tok, width), BF)
    return pl.pallas_call(
        finish_body,
        grid=(steps,),
        out_shape=(seq_out,) * 4 + (jax.ShapeDtypeStruct((chan, lags), F32),),
        in_specs=[seq] * 4 + [seq_t] * 2 + [filt],
        out_specs=(seq,) * 4 + (filt,),
        compiler_params=pltpu.CompilerParams(vmem_limit_bytes=58 * 1024 * 1024),
    )(q, g, k, v, conv_t, gs_t, grad_filters)


def solution(mesh):
    n_ctx, n_tp = mesh.shape["ctx"], mesh.shape["tp"]

    def per_device(query_rows, key_rows, value_rows, positions, filters, bias_term, grad_out):
        width = query_rows.shape[1]
        slot = query_rows.shape[0] // n_ctx
        tok = grad_out.shape[0] * n_tp
        chan = filters.shape[0]
        (wf_hi, wf_lo), (wi_hi, wi_lo), cos, sin = make_tables(n_ctx, tok)
        bins = n_ctx + 1
        vm = pltpu.VMEM
        rows_bf = vm((n_ctx * slot, width), BF)
        seq = vm((tok, width), BF)
        seq_t = vm((width, tok), BF)
        parts = vm((n_ctx, chan, tok), BF)
        spec = vm((bins * chan, 2 * tok), F32)
        half_spec = vm((bins * chan, 2 * tok), BF)
        table = vm((2 * tok, 2 * tok), BF)
        any_spec = pl.BlockSpec(memory_space=pl.ANY)
        vmem_spec = pl.BlockSpec(memory_space=pltpu.VMEM)
        seq_out = jax.ShapeDtypeStruct((tok, width), BF)

        def body(*refs):
            kernel_body((n_ctx, n_tp, tok, slot, chan), *refs)

        seq_t_out = jax.ShapeDtypeStruct((width, tok), BF)

        parts_out = pl.pallas_call(
            body,
            out_shape=(seq_out,) * 4 + (seq_t_out,) * 2 + (jax.ShapeDtypeStruct(filters.shape, F32),),
            in_specs=[any_spec] * 9 + [vmem_spec] * 4,
            out_specs=(any_spec,) * 7,
            scratch_shapes=[
                rows_bf, rows_bf, rows_bf, seq, vm(filters.shape, F32), table, table, table, table,
                vm((tok, n_ctx * slot), BF), seq, seq, seq, seq_t, seq_t, parts, parts,
                half_spec, half_spec, spec, spec, spec, spec,
                parts, parts, vm(filters.shape, F32), vm((chan, 128), F32),
                pltpu.SemaphoreType.DMA((8,)),
                pltpu.SemaphoreType.DMA((8,)),
                pltpu.SemaphoreType.DMA((5,)),
                pltpu.SemaphoreType.DMA((5,)),
            ],
            compiler_params=pltpu.CompilerParams(
                collective_id=0, has_side_effects=True, vmem_limit_bytes=58 * 1024 * 1024
            ),
        )(
            query_rows, key_rows, value_rows, grad_out, filters,
            wf_hi, wf_lo, wi_hi, wi_lo,
            positions, bias_term.reshape(1, chan), cos, sin,
        )
        return finish(*parts_out)

    in_specs = (
        P("ctx", "tp"),
        P("ctx", "tp"),
        P("ctx", "tp"),
        P(),
        P(("tp", "ctx"), None),
        P(("tp", "ctx")),
        P(("ctx", "tp"), None),
    )
    out_specs = (
        P("ctx", "tp"),
        P("ctx", "tp"),
        P("ctx", "tp"),
        P("ctx", "tp"),
        P(("tp", "ctx"), None),
    )
    return jax.shard_map(
        per_device, mesh=mesh, in_specs=in_specs, out_specs=out_specs, check_vma=False
    )
```

```python
import math

import jax
import jax.numpy as jnp
import numpy as np
from jax import lax
from jax.experimental import pallas as pl
from jax.experimental.pallas import tpu as pltpu
from jax.sharding import PartitionSpec as P

MESH = pl.DeviceIdType.MESH
BF = jnp.bfloat16
F32 = jnp.float32
FAR_FIRST = (10, 5, 15, 13, 7, 14, 6, 11, 9, 2, 8, 1, 12, 3, 4)


def split_bf16(table):
    high = table.astype(jnp.bfloat16)
    low = (table - high.astype(np.float64)).astype(jnp.bfloat16)
    return high, low


def make_tables(shards, tokens):
    length = 2 * shards * tokens
    r = np.arange(tokens)
    inner = 2.0 * math.pi * ((r[:, None] * r[None, :]) % tokens) / tokens
    cos, sin = np.cos(inner), np.sin(inner)
    forward = np.block([[cos, -sin], [sin, cos]])
    backward = np.block([[cos, sin], [-sin, cos]])
    k = np.arange(shards + 1)
    twist = 2.0 * math.pi * (k[:, None] * r[None, :]) / length
    return (
        split_bf16(forward),
        split_bf16(backward),
        np.cos(twist).astype(np.float32),
        np.sin(twist).astype(np.float32),
    )


def real_dft_padded(xs):
    half = len(xs)
    if half == 1:
        return [(xs[0], None), (xs[0], None)]
    even = real_dft_padded(xs[0::2])
    odd = real_dft_padded(xs[1::2])
    out = [None] * (half + 1)
    out[0] = (even[0][0] + odd[0][0], None)
    out[half] = (even[0][0] - odd[0][0], None)
    mid = half // 2
    for k in range(1, mid):
        angle = math.pi * k / half
        c, s = math.cos(angle), math.sin(angle)
        o_re, o_im = odd[k]
        t_re = o_re * c + o_im * s
        t_im = o_im * c - o_re * s
        e_re, e_im = even[k]
        out[k] = (e_re + t_re, e_im + t_im)
        out[half - k] = (e_re - t_re, t_im - e_im)
    out[mid] = (even[mid][0], -odd[mid][0])
    return out


def real_inverse_half(bins):
    half = len(bins) - 1
    if half == 1:
        return [bins[0][0] + bins[1][0]]
    mid = half // 2
    even = [None] * (mid + 1)
    odd = [None] * (mid + 1)
    even[0] = (bins[0][0] + bins[half][0], None)
    odd[0] = (bins[0][0] - bins[half][0], None)
    for k in range(1, mid):
        angle = math.pi * k / half
        c, s = math.cos(angle), math.sin(angle)
        a_re, a_im = bins[k]
        b_re, b_im = bins[half - k]
        even[k] = (a_re + b_re, a_im - b_im)
        d_re, d_im = a_re - b_re, a_im + b_im
        odd[k] = (d_re * c - d_im * s, d_im * c + d_re * s)
    m_re, m_im = bins[mid]
    even[mid] = (m_re + m_re, None)
    odd[mid] = (-(m_im + m_im), None)
    y_even = real_inverse_half(even)
    y_odd = real_inverse_half(odd)
    out = [None] * half
    out[0::2] = y_even
    out[1::2] = y_odd
    return out


def kernel_body(
    sizes,
    q_hbm, k_hbm, v_hbm, g_hbm, f_hbm, wf_hi_hbm, wf_lo_hbm, wi_hi_hbm, wi_lo_hbm,
    positions_ref, bias_row, cos_ref, sin_ref,
    q_out, g_out, k_out, v_out, conv_t, gs_t, f_out,
    rq, rk, rv, gtok, f_buf, wf_hi, wf_lo, wi_hi, wi_lo,
    hot, q_seq, k_seq, v_seq, sig_t, gc_t, sig_in, gc_in,
    l_hi, l_lo, spec_f, spec_s, spec_g, z_buf,
    conv_o, gs_o, gf_ref, bias_ref,
    recv_sem, send_sem, local_sem, out_sem,
):
    n_ctx, n_tp, tok, slot, chan = sizes
    side = 4
    width = n_ctx * chan
    me = lax.axis_index("ctx")
    my_tp = lax.axis_index("tp")
    my_y, my_x = me // side, me % side
    factor = 1.0 / math.sqrt(n_ctx * tok)
    inv_len = 1.0 / (2 * n_ctx * tok)
    bins = n_ctx + 1

    def partner(o):
        return ((my_y + o // side) % side) * side + (my_x + o % side) % side

    def each_partner(fn):
        for o in FAR_FIRST:
            fn(partner(o))

    loads = [
        pltpu.make_async_copy(src, dst, local_sem.at[n])
        for n, (src, dst) in enumerate(
            ((f_hbm, f_buf), (wf_hi_hbm, wf_hi), (wf_lo_hbm, wf_lo), (wi_hi_hbm, wi_hi), (wi_lo_hbm, wi_lo))
        )
    ]
    for copy in loads:
        copy.start()

    barrier = pltpu.get_barrier_semaphore()
    each_partner(
        lambda d: pl.semaphore_signal(barrier, inc=1, device_id=(d, my_tp), device_id_type=MESH)
    )
    lax.fori_loop(
        1,
        n_tp,
        lambda o, c: (
            pl.semaphore_signal(
                barrier, inc=1, device_id=(me, (my_tp + o) % n_tp), device_id_type=MESH
            ),
            c,
        )[1],
        0,
    )
    pl.semaphore_wait(barrier, n_ctx + n_tp - 2)

    def send_rows(src, dst, n):
        def one(d):
            pltpu.make_async_remote_copy(
                src_ref=src.at[pl.ds(pl.multiple_of(d * slot, slot), slot), :],
                dst_ref=dst.at[pl.ds(pl.multiple_of(me * slot, slot), slot), :],
                send_sem=send_sem.at[n],
                recv_sem=recv_sem.at[n],
                device_id=(d, my_tp),
                device_id_type=MESH,
            ).start()

        own = pl.ds(pl.multiple_of(me * slot, slot), slot)
        pltpu.make_async_copy(src.at[own, :], dst.at[own, :], recv_sem.at[n]).start()
        each_partner(one)

    send_rows(k_hbm, rk, 0)
    send_rows(v_hbm, rv, 1)

    def send_grad(o, carry):
        d = (my_tp + o) % n_tp
        pltpu.make_async_remote_copy(
            src_ref=g_hbm.at[:, pl.ds(pl.multiple_of(d * width, width), width)],
            dst_ref=gtok.at[pl.ds(pl.multiple_of(my_tp * slot, slot), slot), :],
            send_sem=send_sem.at[3],
            recv_sem=recv_sem.at[3],
            device_id=(me, d),
            device_id_type=MESH,
        ).start()
        return carry

    pltpu.make_async_copy(
        g_hbm.at[:, pl.ds(pl.multiple_of(my_tp * width, width), width)],
        gtok.at[pl.ds(pl.multiple_of(my_tp * slot, slot), slot), :],
        recv_sem.at[3],
    ).start()
    lax.fori_loop(1, n_tp, send_grad, 0)
    send_rows(q_hbm, rq, 2)

    rows_all = n_ctx * slot
    lane = lax.broadcasted_iota(jnp.int32, (rows_all, rows_all), 1)
    column = lax.broadcasted_iota(jnp.int32, (rows_all, rows_all), 0)
    pick = jnp.where(column == me * slot + lane % slot, 1.0, 0.0).astype(BF)
    mine = jnp.dot(
        positions_ref[...].astype(F32).astype(BF), pick, preferred_element_type=F32
    )
    buffer = lax.broadcasted_iota(jnp.int32, mine.shape, 0)
    keep = lax.broadcasted_iota(jnp.int32, mine.shape, 1) // slot == buffer
    slots = jnp.sum(jnp.where(keep, mine, 0.0), axis=0, keepdims=True).astype(jnp.int32)
    bias_ref[...] = jnp.broadcast_to(bias_row[...], (128, chan)).T
    hot[...] = jnp.where(
        slots == lax.broadcasted_iota(jnp.int32, hot.shape, 0), 1.0, 0.0
    ).astype(BF)

    row_step, lane_step = 16, 128
    halves = tok // lane_step
    pieces = (chan // row_step) * halves

    def place(it):
        rows = pl.multiple_of((it // halves) * row_step, row_step)
        lanes = pl.multiple_of((it % halves) * lane_step, lane_step)
        return rows, lanes

    def put_split(row, lane, value, exact):
        high = value.astype(BF)
        at = (pl.ds(pl.multiple_of(row, row_step), row_step), pl.ds(pl.multiple_of(lane, lane_step), lane_step))
        l_hi[at] = high
        if exact:
            l_lo[at] = (value - high.astype(F32)).astype(BF)

    def forward_outer(load, exact):
        def step(it, carry):
            rows, lanes = place(it)
            spectrum = real_dft_padded([load(j, rows, lanes) for j in range(n_ctx)])
            for k in range(bins):
                re, im = spectrum[k]
                if k == 0:
                    put_split(rows, lanes, re, exact)
                    put_split(rows, tok + lanes, jnp.zeros_like(re), exact)
                    continue
                c = cos_ref[k : k + 1, pl.ds(lanes, lane_step)]
                s = sin_ref[k : k + 1, pl.ds(lanes, lane_step)]
                if im is None:
                    t_re, t_im = re * c, -(re * s)
                else:
                    t_re, t_im = re * c + im * s, im * c - re * s
                put_split(k * chan + rows, lanes, t_re, exact)
                put_split(k * chan + rows, tok + lanes, t_im, exact)
            return carry

        lax.fori_loop(0, pieces, step, 0)

    total_rows = bins * chan
    block_rows = total_rows // 4

    def inner(high, low, dest, exact):
        def step(m, carry):
            at = pl.ds(pl.multiple_of(m * block_rows, row_step), block_rows)
            a = l_hi[at, :]
            total = jnp.dot(a, high[...], preferred_element_type=F32)
            if exact:
                total += jnp.dot(a, low[...], preferred_element_type=F32)
                total += jnp.dot(l_lo[at, :], high[...], preferred_element_type=F32)
            dest[at, :] = total
            return carry

        lax.fori_loop(0, 4, step, 0)

    def multiply(one, two, conjugate_one, exact):
        def step(m, carry):
            row = m * row_step
            at = pl.ds(pl.multiple_of(row, row_step), row_step)
            for lane in range(0, tok, lane_step):
                re_at, im_at = slice(lane, lane + lane_step), slice(tok + lane, tok + lane + lane_step)
                a, b = one[at, re_at], one[at, im_at]
                c, d = two[at, re_at], two[at, im_at]
                if conjugate_one:
                    re, im = a * c + b * d, a * d - b * c
                else:
                    re, im = a * c - b * d, a * d + b * c
                put_split(row, lane, re, exact)
                put_split(row, tok + lane, im, exact)
            return carry

        lax.fori_loop(0, total_rows // row_step, step, 0)

    def product_inner(one, two, conjugate_one):
        def step(m, carry):
            at = pl.ds(pl.multiple_of(m * block_rows, row_step), block_rows)
            a, b = one[at, :tok], one[at, tok:]
            c, d = two[at, :tok], two[at, tok:]
            if conjugate_one:
                re, im = a * c + b * d, a * d - b * c
            else:
                re, im = a * c - b * d, a * d + b * c
            z_buf[at, :] = jnp.dot(
                re.astype(BF), wi_hi[:tok, :], preferred_element_type=F32
            ) + jnp.dot(im.astype(BF), wi_hi[tok:, :], preferred_element_type=F32)
            return carry

        lax.fori_loop(0, 4, step, 0)

    def inverse_outer(store, middle=None):
        def step(it, carry):
            rows, lanes = place(it)
            spectrum = []
            for k in range(bins):
                at = pl.ds(pl.multiple_of(k * chan + rows, row_step), row_step)
                re = z_buf[at, pl.ds(lanes, lane_step)]
                if k == 0:
                    spectrum.append((re, None))
                    continue
                im = z_buf[at, pl.ds(pl.multiple_of(tok + lanes, lane_step), lane_step)]
                c = cos_ref[k : k + 1, pl.ds(lanes, lane_step)]
                s = sin_ref[k : k + 1, pl.ds(lanes, lane_step)]
                if k == n_ctx:
                    spectrum.append((re * c - im * s, None))
                else:
                    spectrum.append((re * c - im * s, im * c + re * s))
            for j, y in enumerate(real_inverse_half(spectrum)):
                store(j, rows, lanes, y * (factor * inv_len))
            return carry

        lax.fori_loop(0, pieces // 2, step, 0)
        if middle is not None:
            middle()
        lax.fori_loop(pieces // 2, pieces, step, 0)

    for copy in loads:
        copy.wait()
    forward_outer(
        lambda j, rows, lanes: f_buf[
            pl.ds(rows, row_step), pl.ds(pl.multiple_of(j * tok + lanes, lane_step), lane_step)
        ],
        True,
    )
    inner(wf_hi, wf_lo, spec_f, True)

    def wait_all(buf, n):
        pltpu.make_async_copy(buf, buf, recv_sem.at[n]).wait()

    def hand_out(src, dst, n):
        pltpu.make_async_copy(src, dst, out_sem.at[n]).start()

    def settled(rows_ref, cols):
        return jnp.dot(hot[...], rows_ref[:, cols], preferred_element_type=F32)

    group = side * chan

    def send_channels(src, dst, n, y):
        for dx in (2, 1, 3, 0):
            d = y * side + (my_x + dx) % side
            at = pl.ds(pl.multiple_of(d * chan, chan), chan)
            pl.when(d != me)(
                lambda: pltpu.make_async_remote_copy(
                    src_ref=src.at[at, :],
                    dst_ref=dst.at[me],
                    send_sem=send_sem.at[n],
                    recv_sem=recv_sem.at[n],
                    device_id=(d, my_tp),
                    device_id_type=MESH,
                ).start()
            )

    def send_own_channels(src, dst, n):
        at = pl.ds(pl.multiple_of(me * chan, chan), chan)
        pltpu.make_async_copy(src.at[at, :], dst.at[me], recv_sem.at[n]).start()

    wait_all(rk, 0)
    wait_all(rv, 1)

    def signal_step(i, carry):
        y = (my_y + i + 1) % side
        cols = pl.ds(pl.multiple_of(y * group, group), group)
        key = settled(rk, cols)
        value = settled(rv, cols)
        k_seq[:, cols] = key.astype(BF)
        v_seq[:, cols] = value.astype(BF)
        sig_t[cols, :] = (key * value).T.astype(BF)
        send_channels(sig_t, sig_in, 4, y)
        return carry

    lax.fori_loop(0, side, signal_step, 0)
    send_own_channels(sig_t, sig_in, 4)
    hand_out(k_seq, k_out, 0)
    hand_out(v_seq, v_out, 1)

    wait_all(rq, 2)
    wait_all(gtok, 3)

    def grad_step(i, carry):
        y = (my_y + i + 1) % side
        cols = pl.ds(pl.multiple_of(y * group, group), group)
        query = settled(rq, cols)
        q_seq[:, cols] = query.astype(BF)
        gc_t[cols, :] = (query * gtok[:, cols].astype(F32)).T.astype(BF)
        send_channels(gc_t, gc_in, 5, y)
        return carry

    lax.fori_loop(0, side, grad_step, 0)
    send_own_channels(gc_t, gc_in, 5)
    hand_out(q_seq, q_out, 2)
    hand_out(gtok, g_out, 3)

    half_chan = chan // 2

    def send_tokens(src, dst, n, part):
        from_rows = pl.ds(part * half_chan, half_chan)
        at = pl.ds(pl.multiple_of(me * chan + part * half_chan, half_chan), half_chan)

        def one(d):
            pltpu.make_async_remote_copy(
                src_ref=src.at[d, from_rows, :],
                dst_ref=dst.at[at, :],
                send_sem=send_sem.at[n],
                recv_sem=recv_sem.at[n],
                device_id=(d, my_tp),
                device_id_type=MESH,
            ).start()

        pltpu.make_async_copy(src.at[me, from_rows, :], dst.at[at, :], recv_sem.at[n]).start()
        each_partner(one)

    def piece(buf, j, rows, lanes):
        return buf[j, pl.ds(rows, row_step), pl.ds(lanes, lane_step)].astype(F32)

    def store_with_bias(direct, dest):
        def store(j, rows, lanes, y):
            bias = bias_ref[pl.ds(rows, row_step), :]
            dest[j, pl.ds(rows, row_step), pl.ds(lanes, lane_step)] = (
                bias * piece(direct, j, rows, lanes) + y
            ).astype(BF)

        return store

    wait_all(sig_in, 4)
    forward_outer(lambda j, rows, lanes: piece(sig_in, j, rows, lanes), False)
    inner(wf_hi, wf_lo, spec_s, False)
    product_inner(spec_f, spec_s, False)
    inverse_outer(store_with_bias(sig_in, conv_o), lambda: send_tokens(conv_o, conv_t, 6, 0))
    send_tokens(conv_o, conv_t, 6, 1)

    wait_all(gc_in, 5)
    forward_outer(lambda j, rows, lanes: piece(gc_in, j, rows, lanes), False)
    inner(wf_hi, wf_lo, spec_g, False)
    product_inner(spec_f, spec_g, True)
    inverse_outer(store_with_bias(gc_in, gs_o), lambda: send_tokens(gs_o, gs_t, 7, 0))
    send_tokens(gs_o, gs_t, 7, 1)

    multiply(spec_s, spec_g, True, True)
    inner(wi_hi, wi_lo, z_buf, True)

    def store_filter(j, rows, lanes, y):
        gf_ref[pl.ds(rows, row_step), pl.ds(pl.multiple_of(j * tok + lanes, lane_step), lane_step)] = y

    inverse_outer(store_filter)

    hand_out(gf_ref, f_out, 4)

    wait_all(conv_o, 6)
    wait_all(gs_o, 7)
    for n, (src, dst) in enumerate(
        ((k_seq, k_out), (v_seq, v_out), (q_seq, q_out), (gtok, g_out), (gf_ref, f_out))
    ):
        pltpu.make_async_copy(src, dst, out_sem.at[n]).wait()

    def wait_sent(buf, n):
        pltpu.make_async_copy(buf, buf, send_sem.at[n]).wait()

    rows_sent = pl.ds(0, (n_ctx - 1) * slot)
    wait_sent(rk.at[rows_sent, :], 0)
    wait_sent(rv.at[rows_sent, :], 1)
    wait_sent(rq.at[rows_sent, :], 2)
    wait_sent(gtok.at[pl.ds(0, (n_tp - 1) * slot), :], 3)
    parts_sent = pl.ds(0, n_ctx - 1)
    wait_sent(sig_in.at[parts_sent], 4)
    wait_sent(gc_in.at[parts_sent], 5)
    wait_sent(conv_o.at[parts_sent], 6)
    wait_sent(gs_o.at[parts_sent], 7)


def finish_body(q, g, k, v, conv_t, gs_t, f_in, out, gq, gk, gv, f_out):
    conv = conv_t[...].astype(F32).T
    out[...] = (q[...].astype(F32) * conv).astype(BF)
    gq[...] = (g[...].astype(F32) * conv).astype(BF)
    grad = gs_t[...].astype(F32).T
    gk[...] = (grad * v[...].astype(F32)).astype(BF)
    gv[...] = (grad * k[...].astype(F32)).astype(BF)
    f_out[...] = f_in[...]


def finish(q, g, k, v, conv_t, gs_t, grad_filters):
    tok, width = q.shape
    chan, lags = grad_filters.shape
    steps = 2
    seq = pl.BlockSpec((tok, width // steps), lambda i: (0, i))
    seq_t = pl.BlockSpec((width // steps, tok), lambda i: (i, 0))
    filt = pl.BlockSpec((chan // steps, lags), lambda i: (i, 0))
    seq_out = jax.ShapeDtypeStruct((tok, width), BF)
    return pl.pallas_call(
        finish_body,
        grid=(steps,),
        out_shape=(seq_out,) * 4 + (jax.ShapeDtypeStruct((chan, lags), F32),),
        in_specs=[seq] * 4 + [seq_t] * 2 + [filt],
        out_specs=(seq,) * 4 + (filt,),
        compiler_params=pltpu.CompilerParams(vmem_limit_bytes=58 * 1024 * 1024),
    )(q, g, k, v, conv_t, gs_t, grad_filters)


def solution(mesh):
    n_ctx, n_tp = mesh.shape["ctx"], mesh.shape["tp"]

    def per_device(query_rows, key_rows, value_rows, positions, filters, bias_term, grad_out):
        width = query_rows.shape[1]
        slot = query_rows.shape[0] // n_ctx
        tok = grad_out.shape[0] * n_tp
        chan = filters.shape[0]
        (wf_hi, wf_lo), (wi_hi, wi_lo), cos, sin = make_tables(n_ctx, tok)
        bins = n_ctx + 1
        vm = pltpu.VMEM
        rows_bf = vm((n_ctx * slot, width), BF)
        seq = vm((tok, width), BF)
        seq_t = vm((width, tok), BF)
        parts = vm((n_ctx, chan, tok), BF)
        spec = vm((bins * chan, 2 * tok), F32)
        half_spec = vm((bins * chan, 2 * tok), BF)
        table = vm((2 * tok, 2 * tok), BF)
        any_spec = pl.BlockSpec(memory_space=pl.ANY)
        vmem_spec = pl.BlockSpec(memory_space=pltpu.VMEM)
        seq_out = jax.ShapeDtypeStruct((tok, width), BF)

        def body(*refs):
            kernel_body((n_ctx, n_tp, tok, slot, chan), *refs)

        seq_t_out = jax.ShapeDtypeStruct((width, tok), BF)

        parts_out = pl.pallas_call(
            body,
            out_shape=(seq_out,) * 4 + (seq_t_out,) * 2 + (jax.ShapeDtypeStruct(filters.shape, F32),),
            in_specs=[any_spec] * 9 + [vmem_spec] * 4,
            out_specs=(any_spec,) * 7,
            scratch_shapes=[
                rows_bf, rows_bf, rows_bf, seq, vm(filters.shape, F32), table, table, table, table,
                vm((tok, n_ctx * slot), BF), seq, seq, seq, seq_t, seq_t, parts, parts,
                half_spec, half_spec, spec, spec, spec, spec,
                parts, parts, vm(filters.shape, F32), vm((chan, 128), F32),
                pltpu.SemaphoreType.DMA((8,)),
                pltpu.SemaphoreType.DMA((8,)),
                pltpu.SemaphoreType.DMA((5,)),
                pltpu.SemaphoreType.DMA((5,)),
            ],
            compiler_params=pltpu.CompilerParams(
                collective_id=0, has_side_effects=True, vmem_limit_bytes=58 * 1024 * 1024
            ),
        )(
            query_rows, key_rows, value_rows, grad_out, filters,
            wf_hi, wf_lo, wi_hi, wi_lo,
            positions, bias_term.reshape(1, chan), cos, sin,
        )
        return finish(*parts_out)

    in_specs = (
        P("ctx", "tp"),
        P("ctx", "tp"),
        P("ctx", "tp"),
        P(),
        P(("tp", "ctx"), None),
        P(("tp", "ctx")),
        P(("ctx", "tp"), None),
    )
    out_specs = (
        P("ctx", "tp"),
        P("ctx", "tp"),
        P("ctx", "tp"),
        P("ctx", "tp"),
        P(("tp", "ctx"), None),
    )
    return jax.shard_map(
        per_device, mesh=mesh, in_specs=in_specs, out_specs=out_specs, check_vma=False
    )
```
